128 devices in a mesh: lat: 128 (over y, x, z, core).
Axes of the slice: x: 4, y: 4, z: 4, core: 2. Of those that a mesh axis runs over, the one named last changes fastest.
Arguments:
- features: bfloat16 [256, 32, 8192], P('lat'), may hold values from -6 to 6
- cotangent: bfloat16 [256, 32, 8192], P('lat'), may hold values from -18 to 18
- basis_table: bfloat16 [256, 9, 9, 9], P('lat'), may hold values from -1.75 to 1.75
- lon_reach: int32 [256, 9], P('lat'), may hold values from 0 to 4, as said below
- weights: bfloat16 [9, 32, 32], replicated, may hold values from -0.375 to 0.375
Outputs:
- grad_input: bfloat16 [256, 32, 8192], P('lat')
- grad_weight: float32 [9, 32, 32], replicated
The draws below stay inside these ranges and needn't reach their ends.
Inputs may be any that keep to these rules, and one draw needn't show every extreme that they name: `lon_reach`: entry 4 (the output cycle's own cycle) of every cycle is 4.
All inputs are finite; a program needn't handle non-finite values.
Results may differ from the reference program's by a relative error of at most 0.0065.
Values may be sent and summed in bfloat16 or wider, within the bound.
No kernel may reach another device: no remote copies, remote signals or barrier semaphores. Data moves between devices by JAX's collectives and lax.ppermute only.
A program may use at most 128 MiB of HBM per device.

```python
import math
import jax
import jax.numpy as jnp
from jax import lax

C = 32
K = 9
LON = 8192
RAD = 4
LON_HALF = 4
TAPS = 9
TAPS_L = 9
CYCLES = 256


def draw_cotangent(key, part):
    cycle_pos = jnp.arange(CYCLES, dtype=jnp.float32)[:, None, None] / CYCLES
    base = jnp.clip(jax.random.normal(jax.random.fold_in(key, 11), (CYCLES, C, LON), jnp.float32), -6.0, 6.0)
    return (base * (0.5 + cycle_pos)).astype(jnp.bfloat16)


def draw_lon_reach(key, part):
    values = jax.random.randint(jax.random.fold_in(key, 23), (CYCLES, TAPS), 0, LON_HALF + 1, dtype=jnp.int32)
    centre = (jnp.arange(TAPS, dtype=jnp.int32) == RAD)[None, :]
    return jnp.where(centre, jnp.int32(LON_HALF), values).astype(jnp.int32)


def levels(own_key, shape, pieces, smallest, largest):
    loudness = 1.0
    for axis_at, shards_of in pieces:
        steps = jax.random.uniform(jax.random.fold_in(jax.random.fold_in(own_key, 6), axis_at), (shards_of,), jnp.float32, smallest / len(pieces), largest / len(pieces))
        loudness = loudness * jnp.repeat(jnp.exp(steps), shape[axis_at] // shards_of).reshape((-1,) + (1,) * (len(shape) - 1 - axis_at))
    return loudness


def centred(key, dims, scale, limit, shards=(), kind=jnp.bfloat16):
    array = jax.random.normal(key, dims, jnp.float32) * scale
    if len(shards) > 0:
        array = levels(key, dims, shards, -0.22, 0.18) * array
    return jnp.clip(array, min=-limit, max=limit).astype(kind)


def setup_inputs(seed: int = 0) -> dict:
    streams_of = jax.random.split(jax.random.key(seed), 6)
    return {
        "features": centred(streams_of[0], (CYCLES, C, LON), 1.0, 6.0, ((0, 128),)),
        "cotangent": draw_cotangent(jax.random.fold_in(streams_of[5], 71), 0),
        "basis_table": centred(streams_of[2], (CYCLES, TAPS, TAPS_L, K), 0.111, 1.75, ((0, 128),)),
        "lon_reach": draw_lon_reach(jax.random.fold_in(streams_of[5], 71), 0),
        "weights": centred(streams_of[4], (K, C, C), (C * K) ** -0.5, 0.375),
    }


def reference(features, cotangent, basis_table, lon_reach, weights):
    cycle_taps = 2 * RAD + 1
    lon_taps = 2 * LON_HALF + 1
    offsets_lon = jnp.arange(lon_taps, dtype=jnp.int32) - LON_HALF
    inside = (jnp.abs(offsets_lon)[None, None, :] <= lon_reach[:, :, None]).astype(jnp.float32)
    masked = basis_table.astype(jnp.float32) * inside[..., None]
    filt = jnp.einsum('rjdk,koi->rjdoi', masked, weights.astype(jnp.float32)).astype(jnp.bfloat16)
    padded = jnp.pad(features, ((RAD, RAD), (0, 0), (0, 0)))

    def step(carry, cycle_index):
        summed, grad_w = carry
        window = lax.dynamic_slice_in_dim(padded, cycle_index, cycle_taps, 0).astype(jnp.float32)
        stacked = jnp.stack([jnp.roll(window, -(column - LON_HALF), axis=-1) for column in range(lon_taps)], axis=1)
        filt_cycle = lax.dynamic_index_in_dim(filt, cycle_index, 0, False).astype(jnp.float32)
        basis_cycle = lax.dynamic_index_in_dim(masked, cycle_index, 0, False)
        pre_act = jnp.einsum('jdoi,jdip->op', filt_cycle, stacked)
        sigmoid_v = jax.nn.sigmoid(pre_act)
        cot_cycle = lax.dynamic_index_in_dim(cotangent, cycle_index, 0, False).astype(jnp.float32)
        delta = (cot_cycle * sigmoid_v * (1.0 + pre_act * (1.0 - sigmoid_v))).astype(jnp.bfloat16)
        delta = lax.optimization_barrier(delta).astype(jnp.float32)
        correl = jnp.einsum('op,jdip->jdoi', delta, stacked)
        grad_w = grad_w + jnp.einsum('jdk,jdoi->koi', basis_cycle, correl)
        rolled = jnp.stack([jnp.roll(delta, column - LON_HALF, axis=-1) for column in range(lon_taps)], axis=0)
        contrib = jnp.einsum('jdoi,dop->jip', filt_cycle, rolled)
        current = lax.dynamic_slice_in_dim(summed, cycle_index, cycle_taps, 0)
        summed = lax.dynamic_update_slice_in_dim(summed, current + contrib, cycle_index, 0)
        return ((summed, grad_w), None)
    initial = (jnp.zeros((CYCLES + 2 * RAD, C, LON), jnp.float32), jnp.zeros((K, C, C), jnp.float32))
    (summed, grad_w), _ = lax.scan(step, initial, jnp.arange(CYCLES, dtype=jnp.int32))
    grad_input = summed[RAD:RAD + CYCLES].astype(jnp.bfloat16)
    return (grad_input, grad_w * (1.0 / math.sqrt(CYCLES * LON)))
```

```python
import functools
import math

import jax
import jax.numpy as jnp
from jax import lax
from jax.experimental import pallas as pl
from jax.experimental.pallas import tpu as pltpu
from jax.sharding import PartitionSpec as P

C = 32
K = 9
RAD = 4
TAPS = 9
OWN = 2
SPAN = OWN + 2 * RAD
ROWS = SPAN * C
BLOCK = OWN * C
DEEP = 3 * ROWS
OUT = 3 * BLOCK
PAD = 128
LANES = 128
TILE = 1024
VMEM = 56 * 1024 * 1024


def spread_matrix(kind, shape):
    row = lax.broadcasted_iota(jnp.int32, shape, 0)
    lane = lax.broadcasted_iota(jnp.int32, shape, 1)
    hit = (lane // C == row) if kind == "table" else (lane % C == row)
    return jnp.where(hit, 1.0, 0.0).astype(jnp.bfloat16)


def filter_kernel(table_ref, weight_ref, out_ref, table_wide, weight_wide):
    table_wide[...] = jnp.dot(
        table_ref[...],
        spread_matrix("table", (3 * SPAN, DEEP)),
        preferred_element_type=jnp.float32,
    )
    weight_wide[...] = jnp.dot(
        weight_ref[...], spread_matrix("weight", (C, DEEP)), preferred_element_type=jnp.float32
    )
    for group in range(3 * OWN):
        total = jnp.zeros((C, DEEP), jnp.float32)
        for k in range(K):
            at = group * K + k
            total = total + table_wide[at : at + 1, :] * weight_wide[k * C : (k + 1) * C, :]
        out_ref[group * C : (group + 1) * C, :] = total.astype(jnp.bfloat16)


def make_filter(table, weights):
    return pl.pallas_call(
        filter_kernel,
        out_shape=jax.ShapeDtypeStruct((OUT, DEEP), jnp.bfloat16),
        in_specs=[pl.BlockSpec(memory_space=pltpu.VMEM)] * 2,
        out_specs=pl.BlockSpec(memory_space=pltpu.VMEM),
        scratch_shapes=[
            pltpu.VMEM((3 * OWN * K, DEEP), jnp.float32),
            pltpu.VMEM((K * C, DEEP), jnp.float32),
        ],
        compiler_params=pltpu.CompilerParams(vmem_limit_bytes=VMEM),
        name="make_filter",
    )(table, weights)


def window_copies(blocks, x_ref, sems, parity, longitude):
    far_row = pl.multiple_of(BLOCK + 2 * BLOCK * parity, BLOCK)
    mate_row = pl.multiple_of(3 * BLOCK - 2 * BLOCK * parity, BLOCK)
    rows = (0, far_row, 2 * BLOCK, mate_row, 4 * BLOCK)
    tiles = longitude // TILE

    def tile_copies(tile):
        first = pl.multiple_of(tile * TILE, TILE)
        return [
            pltpu.make_async_copy(
                block.at[:, pl.ds(first, TILE)],
                x_ref.at[pl.ds(row, BLOCK), pl.ds(first + PAD, TILE)],
                sems.at[place, tile],
            )
            for place, (block, row) in enumerate(zip(blocks, rows))
        ]

    def edge_copies():
        copies = []
        for place, (block, row) in enumerate(zip(blocks, rows)):
            for side, (source, target) in enumerate(
                ((longitude - PAD, 0), (0, longitude + PAD))
            ):
                copies.append(
                    pltpu.make_async_copy(
                        block.at[:, pl.ds(source, PAD)],
                        x_ref.at[pl.ds(row, BLOCK), pl.ds(target, PAD)],
                        sems.at[place, tiles + side],
                    )
                )
        return copies

    return tile_copies, edge_copies


def pre_shift(x_ref, x3_ref, first):
    wide = x_ref[:, pl.ds(first, TILE + 2 * PAD)]
    for e in range(3):
        start = PAD + e - 1
        x3_ref[e * ROWS : (e + 1) * ROWS, :] = wide[:, start : start + TILE]


def conv_kernel(with_act, matrix_ref, low, far, own, mate, high, *rest):
    if with_act:
        cot_ref, out_ref, x_ref, x3_ref, p3_ref, sems = rest
    else:
        out_ref, x_ref, x3_ref, p3_ref, sems = rest
    longitude = own.shape[1]
    tiles = longitude // TILE
    parity = lax.rem(lax.axis_index("lat"), 2)
    tile_copies, edge_copies = window_copies(
        (low, far, own, mate, high), x_ref, sems, parity, longitude
    )
    for copy in edge_copies():
        copy.start()

    @pl.loop(0, tiles)
    def _(tile):
        for copy in tile_copies(tile):
            copy.start()

    for copy in edge_copies():
        copy.wait()
    for copy in tile_copies(0):
        copy.wait()

    @pl.loop(0, tiles)
    def _(tile):
        @pl.when(tile + 1 < tiles)
        def _():
            for copy in tile_copies(tile + 1):
                copy.wait()

        first = pl.multiple_of(tile * TILE, TILE)
        pre_shift(x_ref, x3_ref, first)
        p3_ref[:, pl.ds(first + PAD, TILE)] = jnp.dot(
            matrix_ref[...], x3_ref[...], preferred_element_type=jnp.float32
        )

    p3_ref[:, 0:PAD] = p3_ref[:, longitude : longitude + PAD]
    p3_ref[:, longitude + PAD : longitude + 2 * PAD] = p3_ref[:, PAD : 2 * PAD]

    @pl.loop(0, tiles)
    def _(tile):
        first = pl.multiple_of(tile * TILE, TILE)
        total = p3_ref[BLOCK : 2 * BLOCK, pl.ds(first + PAD, TILE)]
        for f in (0, 2):
            wide = p3_ref[f * BLOCK : (f + 1) * BLOCK, pl.ds(first, TILE + 2 * PAD)]
            start = PAD + 3 * (f - 1)
            total = total + wide[:, start : start + TILE]
        if with_act:
            cot = cot_ref[:, pl.ds(first, TILE)].astype(jnp.float32)
            sg = jax.nn.sigmoid(total)
            total = cot * sg * (1.0 + total * (1.0 - sg))
        out_ref[:, pl.ds(first, TILE)] = total.astype(out_ref.dtype)


def conv(matrix, blocks, cot=None):
    longitude = blocks[0].shape[1]
    tiles = longitude // TILE
    extra = [] if cot is None else [cot]
    return pl.pallas_call(
        functools.partial(conv_kernel, cot is not None),
        out_shape=jax.ShapeDtypeStruct((BLOCK, longitude), jnp.bfloat16),
        in_specs=[pl.BlockSpec(memory_space=pltpu.VMEM)]
        + [pl.BlockSpec(memory_space=pl.ANY)] * 5
        + [pl.BlockSpec(memory_space=pltpu.VMEM)] * len(extra),
        out_specs=pl.BlockSpec(memory_space=pltpu.VMEM),
        scratch_shapes=[
            pltpu.VMEM((ROWS, longitude + 2 * PAD), jnp.bfloat16),
            pltpu.VMEM((DEEP, TILE), jnp.bfloat16),
            pltpu.VMEM((OUT, longitude + 2 * PAD), jnp.float32),
            pltpu.SemaphoreType.DMA((5, tiles + 2)),
        ],
        compiler_params=pltpu.CompilerParams(vmem_limit_bytes=VMEM),
        cost_estimate=pl.CostEstimate(
            flops=2 * OUT * DEEP * longitude,
            bytes_accessed=7 * BLOCK * longitude * 2,
            transcendentals=0,
        ),
        name="forward_conv" if extra else "input_conv",
    )(matrix, *blocks, *extra)


def weight_kernel(scale, low, far, own, mate, high, delta, table_ref, out_ref, x_ref, x3_ref, d_ref, d3_ref, g_ref, w_ref, table_wide, sems, dsems):
    longitude = own.shape[1]
    tiles = longitude // TILE
    parity = lax.rem(lax.axis_index("lat"), 2)
    tile_copies, edge_copies = window_copies(
        (low, far, own, mate, high), x_ref, sems, parity, longitude
    )
    delta_copies = [
        pltpu.make_async_copy(
            delta.at[:, pl.ds(source, size)], d_ref.at[:, pl.ds(target, size)], dsems.at[at]
        )
        for at, (source, target, size) in enumerate(
            ((0, PAD, longitude), (longitude - PAD, 0, PAD), (0, longitude + PAD, PAD))
        )
    ]
    for copy in edge_copies() + delta_copies:
        copy.start()

    @pl.loop(0, tiles)
    def _(tile):
        for copy in tile_copies(tile):
            copy.start()

    table_wide[...] = jnp.dot(
        table_ref[...],
        spread_matrix("table", (3 * SPAN, DEEP)),
        preferred_element_type=jnp.float32,
    )
    g_ref[...] = jnp.zeros_like(g_ref)
    for copy in edge_copies() + delta_copies:
        copy.wait()
    for copy in tile_copies(0):
        copy.wait()

    @pl.loop(0, tiles)
    def _(tile):
        @pl.when(tile + 1 < tiles)
        def _():
            for copy in tile_copies(tile + 1):
                copy.wait()

        first = pl.multiple_of(tile * TILE, TILE)
        pre_shift(x_ref, x3_ref, first)
        wide = d_ref[:, pl.ds(first, TILE + 2 * PAD)]
        for f in range(3):
            start = PAD - 3 * (f - 1)
            d3_ref[f * BLOCK : (f + 1) * BLOCK, :] = wide[:, start : start + TILE]
        g_ref[...] += lax.dot_general(
            d3_ref[...],
            x3_ref[...],
            (((1,), (1,)), ((), ())),
            preferred_element_type=jnp.float32,
        )

    whole = DEEP // LANES
    for k in range(K):
        total = jnp.zeros((C, DEEP), jnp.float32)
        for group in range(3 * OWN):
            at = group * K + k
            total = total + table_wide[at : at + 1, :] * g_ref[group * C : (group + 1) * C, :]
        narrow = jnp.concatenate(
            [total[:, whole * LANES :], jnp.zeros((C, (whole + 1) * LANES - DEEP), jnp.float32)],
            axis=1,
        )
        for part in range(whole):
            narrow = narrow + total[:, part * LANES : (part + 1) * LANES]
        w_ref[k * C : (k + 1) * C, :] = narrow
    row = lax.broadcasted_iota(jnp.int32, (LANES, LANES), 0)
    lane = lax.broadcasted_iota(jnp.int32, (LANES, LANES), 1)
    result = jnp.zeros((K * C // 4, LANES), jnp.float32)
    for c in range(4):
        fold = jnp.where(lane == c * C + row % C, 1.0, 0.0)
        result = result + jnp.dot(
            w_ref[pl.ds(c, K * C // 4, stride=4), :],
            fold,
            preferred_element_type=jnp.float32,
            precision=lax.Precision.HIGHEST,
        )
    out_ref[...] = result * scale


def weight_part(blocks, delta, table, scale):
    longitude = delta.shape[1]
    tiles = longitude // TILE
    return pl.pallas_call(
        functools.partial(weight_kernel, scale),
        out_shape=jax.ShapeDtypeStruct((K * C // 4, LANES), jnp.float32),
        in_specs=[pl.BlockSpec(memory_space=pl.ANY)] * 6
        + [pl.BlockSpec(memory_space=pltpu.VMEM)],
        out_specs=pl.BlockSpec(memory_space=pltpu.VMEM),
        scratch_shapes=[
            pltpu.VMEM((ROWS, longitude + 2 * PAD), jnp.bfloat16),
            pltpu.VMEM((DEEP, TILE), jnp.bfloat16),
            pltpu.VMEM((BLOCK, longitude + 2 * PAD), jnp.bfloat16),
            pltpu.VMEM((OUT, TILE), jnp.bfloat16),
            pltpu.VMEM((OUT, DEEP), jnp.float32),
            pltpu.VMEM((K * C, LANES), jnp.float32),
            pltpu.VMEM((3 * OWN * K, DEEP), jnp.float32),
            pltpu.SemaphoreType.DMA((5, tiles + 2)),
            pltpu.SemaphoreType.DMA((3,)),
        ],
        compiler_params=pltpu.CompilerParams(vmem_limit_bytes=VMEM),
        cost_estimate=pl.CostEstimate(
            flops=2 * OUT * DEEP * longitude,
            bytes_accessed=6 * BLOCK * longitude * 2,
            transcendentals=0,
        ),
        name="weight_part",
    )(*blocks, delta, table)


def moved(array, by):
    peers = lax.axis_size("lat")
    return lax.ppermute(
        array, "lat", [(i, i + by) for i in range(peers) if 0 <= i + by < peers]
    )


def swapped(array, bit=1):
    return lax.ppermute(array, "lat", [(i, i ^ bit) for i in range(lax.axis_size("lat"))])


def around(own):
    low = moved(own, 2)
    high = moved(own, -2)
    mate = swapped(own)
    parity = lax.rem(lax.axis_index("lat"), 2)
    far = swapped(jnp.where(parity == 0, high, low))
    return low, far, own, mate, high


def as_table(padded):
    parts = padded.reshape(OWN, SPAN, 3, 3, K)
    return jnp.transpose(parts, (2, 0, 4, 3, 1)).reshape(3 * OWN * K, 3 * SPAN)


def forward_table(masked):
    return as_table(
        jnp.stack(
            [
                jnp.pad(masked[r], ((r, SPAN - TAPS - r), (0, 0), (0, 0)))
                for r in range(OWN)
            ]
        )
    )


def input_table(masked_ext):
    q = jnp.arange(OWN)[:, None, None]
    s = jnp.arange(SPAN)[None, :, None]
    j = jnp.arange(TAPS)[None, None, :]
    hit = (j == TAPS - 1 - (s - q))[..., None, None]
    picked = jnp.sum(jnp.where(hit, masked_ext[None], 0).astype(jnp.float32), axis=2)
    return as_table(picked[:, :, ::-1].astype(jnp.bfloat16))


def body(features, cotangent, basis_table, lon_reach, weights):
    longitude = features.shape[2]
    peers = lax.axis_size("lat")
    offsets = jnp.arange(TAPS, dtype=jnp.int32) - RAD
    inside = jnp.abs(offsets)[None, None, :] <= lon_reach[:, :, None]
    masked = jnp.where(inside[..., None], basis_table, jnp.zeros_like(basis_table))

    feat = around(features.reshape(BLOCK, longitude))
    table = forward_table(masked)
    matrix = make_filter(table, weights.reshape(K * C, C))
    masked_ext = jnp.concatenate(
        [moved(masked, 2), moved(masked, 1), masked, moved(masked, -1), moved(masked, -2)], axis=0
    )
    matrix_in = make_filter(
        input_table(masked_ext), jnp.transpose(weights, (0, 2, 1)).reshape(K * C, C)
    )

    delta = conv(matrix, feat, cotangent.reshape(BLOCK, longitude))
    near = around(delta)
    scale = 1.0 / math.sqrt(peers * OWN * longitude)
    total = weight_part(feat, delta, table, scale)
    for bit in (1, 8, 16, 32, 64, 2, 4):
        total = total + swapped(total, bit)
    grad_input = conv(matrix_in, near)
    return grad_input.reshape(OWN, C, longitude), total.reshape(K, C, C)


def solution(mesh):
    in_specs = (
        P("lat", None, None),
        P("lat", None, None),
        P("lat", None, None, None),
        P("lat", None),
        P(),
    )
    out_specs = (P("lat", None, None), P())
    return jax.shard_map(body, mesh=mesh, in_specs=in_specs, out_specs=out_specs, check_vma=False)
```

```python
import functools
import math

import jax
import jax.numpy as jnp
from jax import lax
from jax.experimental import pallas as pl
from jax.experimental.pallas import tpu as pltpu
from jax.sharding import PartitionSpec as P

C = 32
K = 9
RAD = 4
TAPS = 9
OWN = 2
SPAN = OWN + 2 * RAD
ROWS = SPAN * C
BLOCK = OWN * C
DEEP = 3 * ROWS
OUT = 3 * BLOCK
PAD = 128
LANES = 128
TILE = 2048
VMEM = 28 * 1024 * 1024


def spread_matrix(kind, shape):
    row = lax.broadcasted_iota(jnp.int32, shape, 0)
    lane = lax.broadcasted_iota(jnp.int32, shape, 1)
    hit = (lane // C == row) if kind == "table" else (lane % C == row)
    return jnp.where(hit, 1.0, 0.0).astype(jnp.bfloat16)


def filter_kernel(table_ref, weight_ref, out_ref, table_wide, weight_wide):
    table_wide[...] = jnp.dot(
        table_ref[...],
        spread_matrix("table", (3 * SPAN, DEEP)),
        preferred_element_type=jnp.float32,
    )
    weight_wide[...] = jnp.dot(
        weight_ref[...], spread_matrix("weight", (C, DEEP)), preferred_element_type=jnp.float32
    )
    for group in range(3 * OWN):
        total = jnp.zeros((C, DEEP), jnp.float32)
        for k in range(K):
            at = group * K + k
            total = total + table_wide[at : at + 1, :] * weight_wide[k * C : (k + 1) * C, :]
        out_ref[group * C : (group + 1) * C, :] = total.astype(jnp.bfloat16)


def make_filter(table, weights):
    return pl.pallas_call(
        filter_kernel,
        out_shape=jax.ShapeDtypeStruct((OUT, DEEP), jnp.bfloat16),
        in_specs=[pl.BlockSpec(memory_space=pltpu.VMEM)] * 2,
        out_specs=pl.BlockSpec(memory_space=pltpu.VMEM),
        scratch_shapes=[
            pltpu.VMEM((3 * OWN * K, DEEP), jnp.float32),
            pltpu.VMEM((K * C, DEEP), jnp.float32),
        ],
        compiler_params=pltpu.CompilerParams(vmem_limit_bytes=VMEM),
        name="make_filter",
    )(table, weights)


def window_copies(blocks, x_ref, sems, longitude):
    parity = lax.rem(lax.axis_index("lat"), 2)
    far_row = pl.multiple_of(BLOCK + 2 * BLOCK * parity, BLOCK)
    mate_row = pl.multiple_of(3 * BLOCK - 2 * BLOCK * parity, BLOCK)
    rows = (0, far_row, 2 * BLOCK, mate_row, 4 * BLOCK)
    tiles = longitude // TILE

    def copies(source, target, size, at):
        return [
            pltpu.make_async_copy(
                block.at[:, pl.ds(source, size)],
                x_ref.at[pl.ds(row, BLOCK), pl.ds(target, size)],
                sems.at[place, at],
            )
            for place, (block, row) in enumerate(zip(blocks, rows))
        ]

    main = [copies(tile * TILE, tile * TILE + PAD, TILE, tile) for tile in range(tiles)]
    edges = copies(longitude - PAD, 0, PAD, tiles) + copies(0, longitude + PAD, PAD, tiles + 1)
    return main, edges


def start_all(main, edges):
    for copy in main[0] + edges:
        copy.start()
    for some in main[1:]:
        for copy in some:
            copy.start()


def wait_for(copies):
    for copy in copies:
        copy.wait()


def pre_shift(x_ref, x3_ref, first):
    wide = x_ref[:, first : first + TILE + 2 * PAD]
    for e in range(3):
        start = PAD + e - 1
        x3_ref[e * ROWS : (e + 1) * ROWS, :] = wide[:, start : start + TILE]


def conv_kernel(with_act, matrix_ref, low, far, own, mate, high, *rest):
    if with_act:
        cot_ref, out_ref, x_ref, x3_ref, p3_ref, o_ref, sems, out_sems = rest
    else:
        out_ref, x_ref, x3_ref, p3_ref, o_ref, sems, out_sems = rest
    longitude = own.shape[1]
    tiles = longitude // TILE
    main, edges = window_copies((low, far, own, mate, high), x_ref, sems, longitude)
    start_all(main, edges)
    sends = []

    def finish(first, last):
        size = last - first
        total = p3_ref[BLOCK : 2 * BLOCK, first + PAD : last + PAD]
        for f in (0, 2):
            wide = p3_ref[f * BLOCK : (f + 1) * BLOCK, first : last + 2 * PAD]
            start = PAD + 3 * (f - 1)
            total = total + wide[:, start : start + size]
        if with_act:
            cot = cot_ref[:, first:last].astype(jnp.float32)
            sg = jax.nn.sigmoid(total)
            total = cot * sg * (1.0 + total * (1.0 - sg))
        o_ref[:, first:last] = total.astype(o_ref.dtype)

    def send(first, last):
        copy = pltpu.make_async_copy(
            o_ref.at[:, first:last], out_ref.at[:, first:last], out_sems.at[len(sends)]
        )
        copy.start()
        sends.append(copy)

    wait_for(main[0] + edges)
    for tile in range(tiles):
        if tile + 1 < tiles:
            wait_for(main[tile + 1])
        first = tile * TILE
        pre_shift(x_ref, x3_ref.at[tile % 2], first)
        p3_ref[:, first + PAD : first + PAD + TILE] = jnp.dot(
            matrix_ref[...], x3_ref[tile % 2], preferred_element_type=jnp.float32
        )
        if tile == 0:
            p3_ref[:, longitude + PAD :] = p3_ref[:, PAD : 2 * PAD]
        if tile == tiles - 1:
            p3_ref[:, :PAD] = p3_ref[:, longitude : longitude + PAD]
        if tile >= 1:
            ready = (PAD if tile == 1 else first - TILE - PAD, first - PAD)
            finish(*ready)
            send(*ready)
    for ready in ((longitude - TILE - PAD, longitude), (0, PAD)):
        finish(*ready)
        send(*ready)
    wait_for(sends)


def conv(matrix, blocks, cot=None):
    longitude = blocks[0].shape[1]
    tiles = longitude // TILE
    extra = [] if cot is None else [cot]
    return pl.pallas_call(
        functools.partial(conv_kernel, cot is not None),
        out_shape=jax.ShapeDtypeStruct((BLOCK, longitude), jnp.bfloat16),
        in_specs=[pl.BlockSpec(memory_space=pltpu.VMEM)]
        + [pl.BlockSpec(memory_space=pl.ANY)] * 5
        + [pl.BlockSpec(memory_space=pltpu.VMEM)] * len(extra),
        out_specs=pl.BlockSpec(memory_space=pl.ANY),
        scratch_shapes=[
            pltpu.VMEM((ROWS, longitude + 2 * PAD), jnp.bfloat16),
            pltpu.VMEM((2, DEEP, TILE), jnp.bfloat16),
            pltpu.VMEM((OUT, longitude + 2 * PAD), jnp.float32),
            pltpu.VMEM((BLOCK, longitude), jnp.bfloat16),
            pltpu.SemaphoreType.DMA((5, tiles + 2)),
            pltpu.SemaphoreType.DMA((tiles + 1,)),
        ],
        compiler_params=pltpu.CompilerParams(vmem_limit_bytes=VMEM),
        cost_estimate=pl.CostEstimate(
            flops=2 * OUT * DEEP * longitude,
            bytes_accessed=7 * BLOCK * longitude * 2,
            transcendentals=0,
        ),
        name="forward_conv" if extra else "input_conv",
    )(matrix, *blocks, *extra)


def weight_kernel(
    scale, low, far, own, mate, high, delta, table_ref, out_ref,
    x_ref, x3_ref, d_ref, d3_ref, g_ref, w_ref, table_wide, sems, dsems,
):
    longitude = own.shape[1]
    tiles = longitude // TILE
    main, edges = window_copies((low, far, own, mate, high), x_ref, sems, longitude)
    delta_copies = [
        pltpu.make_async_copy(
            delta.at[:, pl.ds(source, size)], d_ref.at[:, pl.ds(target, size)], dsems.at[at]
        )
        for at, (source, target, size) in enumerate(
            ((0, PAD, longitude), (longitude - PAD, 0, PAD), (0, longitude + PAD, PAD))
        )
    ]
    for copy in delta_copies:
        copy.start()
    start_all(main, edges)
    table_wide[...] = jnp.dot(
        table_ref[...],
        spread_matrix("table", (3 * SPAN, DEEP)),
        preferred_element_type=jnp.float32,
    )
    wait_for(main[0] + edges + delta_copies)
    for tile in range(tiles):
        if tile + 1 < tiles:
            wait_for(main[tile + 1])
        first = tile * TILE
        pre_shift(x_ref, x3_ref.at[tile % 2], first)
        wide = d_ref[:, first : first + TILE + 2 * PAD]
        for f in range(3):
            start = PAD - 3 * (f - 1)
            d3_ref[tile % 2, f * BLOCK : (f + 1) * BLOCK, :] = wide[:, start : start + TILE]
        product = lax.dot_general(
            d3_ref[tile % 2],
            x3_ref[tile % 2],
            (((1,), (1,)), ((), ())),
            preferred_element_type=jnp.float32,
        )
        if tile == 0:
            g_ref[...] = product
        else:
            g_ref[...] += product

    whole = DEEP // LANES
    for k in range(K):
        total = jnp.zeros((C, DEEP), jnp.float32)
        for group in range(3 * OWN):
            at = group * K + k
            total = total + table_wide[at : at + 1, :] * g_ref[group * C : (group + 1) * C, :]
        narrow = jnp.concatenate(
            [total[:, whole * LANES :], jnp.zeros((C, (whole + 1) * LANES - DEEP), jnp.float32)],
            axis=1,
        )
        for part in range(whole):
            narrow = narrow + total[:, part * LANES : (part + 1) * LANES]
        w_ref[k * C : (k + 1) * C, :] = narrow
    row = lax.broadcasted_iota(jnp.int32, (LANES, LANES), 0)
    lane = lax.broadcasted_iota(jnp.int32, (LANES, LANES), 1)
    result = jnp.zeros((K * C // 4, LANES), jnp.float32)
    for c in range(4):
        fold = jnp.where(lane == c * C + row % C, 1.0, 0.0)
        result = result + jnp.dot(
            w_ref[pl.ds(c, K * C // 4, stride=4), :],
            fold,
            preferred_element_type=jnp.float32,
            precision=lax.Precision.HIGHEST,
        )
    out_ref[...] = result * scale


def weight_part(blocks, delta, table, scale):
    longitude = delta.shape[1]
    tiles = longitude // TILE
    return pl.pallas_call(
        functools.partial(weight_kernel, scale),
        out_shape=jax.ShapeDtypeStruct((K * C // 4, LANES), jnp.float32),
        in_specs=[pl.BlockSpec(memory_space=pl.ANY)] * 6
        + [pl.BlockSpec(memory_space=pltpu.VMEM)],
        out_specs=pl.BlockSpec(memory_space=pltpu.VMEM),
        scratch_shapes=[
            pltpu.VMEM((ROWS, longitude + 2 * PAD), jnp.bfloat16),
            pltpu.VMEM((2, DEEP, TILE), jnp.bfloat16),
            pltpu.VMEM((BLOCK, longitude + 2 * PAD), jnp.bfloat16),
            pltpu.VMEM((2, OUT, TILE), jnp.bfloat16),
            pltpu.VMEM((OUT, DEEP), jnp.float32),
            pltpu.VMEM((K * C, LANES), jnp.float32),
            pltpu.VMEM((3 * OWN * K, DEEP), jnp.float32),
            pltpu.SemaphoreType.DMA((5, tiles + 2)),
            pltpu.SemaphoreType.DMA((3,)),
        ],
        compiler_params=pltpu.CompilerParams(vmem_limit_bytes=VMEM),
        cost_estimate=pl.CostEstimate(
            flops=2 * OUT * DEEP * longitude,
            bytes_accessed=6 * BLOCK * longitude * 2,
            transcendentals=0,
        ),
        name="weight_part",
    )(*blocks, delta, table)


def moved(array, by):
    peers = lax.axis_size("lat")
    return lax.ppermute(
        array, "lat", [(i, i + by) for i in range(peers) if 0 <= i + by < peers]
    )


def swapped(array, bit=1):
    return lax.ppermute(array, "lat", [(i, i ^ bit) for i in range(lax.axis_size("lat"))])


def around(own, low, high):
    parity = lax.rem(lax.axis_index("lat"), 2)
    far = swapped(jnp.where(parity == 0, high, low))
    mate = swapped(own)
    return low, far, own, mate, high


def chip_tables(masked):
    parity = lax.rem(lax.axis_index("lat"), 2)
    mate = swapped(masked)
    pair = jnp.where(
        parity == 0, jnp.concatenate([masked, mate]), jnp.concatenate([mate, masked])
    )
    whole = jnp.concatenate([moved(pair, 2), pair, moved(pair, -2)])
    return lax.dynamic_slice_in_dim(whole, OWN * parity, SPAN, 0)


def as_table(padded):
    parts = padded.reshape(OWN, SPAN, 3, 3, K)
    return jnp.transpose(parts, (2, 0, 4, 3, 1)).reshape(3 * OWN * K, 3 * SPAN)


def forward_table(masked):
    return as_table(
        jnp.stack(
            [
                jnp.pad(masked[r], ((r, SPAN - TAPS - r), (0, 0), (0, 0)))
                for r in range(OWN)
            ]
        )
    )


def input_table(masked_ext):
    q = jnp.arange(OWN)[:, None, None]
    s = jnp.arange(SPAN)[None, :, None]
    j = jnp.arange(TAPS)[None, None, :]
    hit = (j == TAPS - 1 - (s - q))[..., None, None]
    picked = jnp.sum(jnp.where(hit, masked_ext[None], 0).astype(jnp.float32), axis=2)
    return as_table(picked[:, :, ::-1].astype(jnp.bfloat16))


def body(features, cotangent, basis_table, lon_reach, weights):
    longitude = features.shape[2]
    peers = lax.axis_size("lat")
    offsets = jnp.arange(TAPS, dtype=jnp.int32) - RAD
    inside = jnp.abs(offsets)[None, None, :] <= lon_reach[:, :, None]
    masked = jnp.where(inside[..., None], basis_table, jnp.zeros_like(basis_table))

    own = features.reshape(BLOCK, longitude)
    low, high = moved(own, 2), moved(own, -2)
    table = forward_table(masked)
    matrix = make_filter(table, weights.reshape(K * C, C))
    masked_ext = chip_tables(masked)
    low, high, own, matrix, masked_ext = lax.optimization_barrier(
        (low, high, own, matrix, masked_ext)
    )
    feat = around(own, low, high)
    matrix_in = make_filter(
        input_table(masked_ext), jnp.transpose(weights, (0, 2, 1)).reshape(K * C, C)
    )
    matrix, matrix_in = lax.optimization_barrier((matrix, matrix_in))
    delta = conv(matrix, feat, cotangent.reshape(BLOCK, longitude))

    low, high = moved(delta, 2), moved(delta, -2)
    scale = 1.0 / math.sqrt(peers * OWN * longitude)
    total = weight_part(feat, delta, table, scale)
    for bit in (1, 8, 16, 32, 64):
        total = total + swapped(total, bit)
    low, high, delta, total = lax.optimization_barrier((low, high, delta, total))
    near = around(delta, low, high)
    for bit in (2, 4):
        total = total + swapped(total, bit)
    grad_input = conv(matrix_in, near)
    return grad_input.reshape(OWN, C, longitude), total.reshape(K, C, C)


def solution(mesh):
    in_specs = (
        P("lat", None, None),
        P("lat", None, None),
        P("lat", None, None, None),
        P("lat", None),
        P(),
    )
    out_specs = (P("lat", None, None), P())
    return jax.shard_map(body, mesh=mesh, in_specs=in_specs, out_specs=out_specs, check_vma=False)
```

```python
import functools
import math

import jax
import jax.numpy as jnp
from jax import lax
from jax.experimental import pallas as pl
from jax.experimental.pallas import tpu as pltpu
from jax.sharding import PartitionSpec as P

C = 32
K = 9
RAD = 4
TAPS = 9
OWN = 2
SPAN = OWN + 2 * RAD
CHIP = 2 * OWN
REACH = 3 * CHIP
BLOCK = OWN * C
STEP = 3 * BLOCK
DEEP = 3 * SPAN * C
OUT = 3 * BLOCK
PAD = 128
LANES = 128
VMEM = 24 * 1024 * 1024
SMALL = 8 * 1024 * 1024
LARGE = 58 * 1024 * 1024
ANY = pl.BlockSpec(memory_space=pl.ANY)
LOCAL = pl.BlockSpec(memory_space=pltpu.VMEM)


def core():
    return lax.rem(lax.axis_index("lat"), 2)


def spread_matrix(kind, shape):
    row = lax.broadcasted_iota(jnp.int32, shape, 0)
    lane = lax.broadcasted_iota(jnp.int32, shape, 1)
    hit = (lane // C == row) if kind == "table" else (lane % C == row)
    return jnp.where(hit, 1.0, 0.0).astype(jnp.bfloat16)


def filter_kernel(table_ref, weight_ref, out_ref, table_wide, weight_wide):
    table_wide[...] = jnp.dot(
        table_ref[...],
        spread_matrix("table", (3 * SPAN, DEEP)),
        preferred_element_type=jnp.float32,
    )
    weight_wide[...] = jnp.dot(
        weight_ref[...], spread_matrix("weight", (C, DEEP)), preferred_element_type=jnp.float32
    )
    for group in range(3 * CHIP):
        total = jnp.zeros((C, DEEP), jnp.float32)
        for k in range(K):
            at = group * K + k
            total = total + table_wide[at : at + 1, :] * weight_wide[k * C : (k + 1) * C, :]
        out_ref[group * C : (group + 1) * C, :] = total.astype(jnp.bfloat16)


def make_filter(table, weights):
    return pl.pallas_call(
        filter_kernel,
        out_shape=jax.ShapeDtypeStruct((2 * OUT, DEEP), jnp.bfloat16),
        in_specs=[LOCAL] * 2,
        out_specs=LOCAL,
        scratch_shapes=[
            pltpu.VMEM((3 * CHIP * K, DEEP), jnp.float32),
            pltpu.VMEM((K * C, DEEP), jnp.float32),
        ],
        compiler_params=pltpu.CompilerParams(vmem_limit_bytes=SMALL),
        name="make_filter",
    )(table, weights)


def wait_for(copies):
    for copy in copies:
        copy.wait()


def window_copies(own, mate, target, sems):
    longitude = own.shape[1]
    half = longitude // 2
    copies = []
    for side, (whole, place) in enumerate(((own, core()), (mate, 1 - core()))):
        row = pl.multiple_of(place * BLOCK, BLOCK)
        for at, (source, start, size) in enumerate(
            (
                (core() * half, PAD, half),
                (longitude - PAD - core() * half, 0, PAD),
                (half - core() * half, PAD + half, PAD),
            )
        ):
            copies.append(
                pltpu.make_async_copy(
                    whole.at[:, pl.ds(pl.multiple_of(source, PAD), size)],
                    target.at[pl.ds(row, BLOCK), pl.ds(start, size)],
                    sems.at[side, at],
                )
            )
    return copies


def window_kernel(own, mate, out_ref, sems):
    copies = window_copies(own, mate, out_ref, sems)
    for copy in copies:
        copy.start()
    wait_for(copies)


def chip_window(own, mate):
    return pl.pallas_call(
        window_kernel,
        out_shape=jax.ShapeDtypeStruct((2 * BLOCK, own.shape[1] // 2 + 2 * PAD), own.dtype),
        in_specs=[ANY, ANY],
        out_specs=LOCAL,
        scratch_shapes=[pltpu.SemaphoreType.DMA((2, 3))],
        compiler_params=pltpu.CompilerParams(vmem_limit_bytes=LARGE),
        name="chip_window",
    )(own, mate)


def join_kernel(got, whole, out, sem):
    half = whole.shape[1] // 2
    start = pl.multiple_of((1 - core()) * half, PAD)
    copy = pltpu.make_async_copy(got, out.at[:, pl.ds(start, half)], sem)
    copy.start()
    copy.wait()


def join(got, whole):
    return pl.pallas_call(
        join_kernel,
        out_shape=jax.ShapeDtypeStruct(whole.shape, whole.dtype),
        in_specs=[LOCAL, ANY],
        out_specs=ANY,
        scratch_shapes=[pltpu.SemaphoreType.DMA],
        input_output_aliases={1: 0},
        compiler_params=pltpu.CompilerParams(vmem_limit_bytes=VMEM),
        name="join",
    )(got, whole)


def in_parts(width):
    cut = width // 2 + PAD
    return ((0, cut), (cut, width - cut))


def chip_copies(blocks, width, x_ref, sems, start):
    cut = width // 2 + PAD
    return [
        [
            pltpu.make_async_copy(
                block.at[:, first : first + size],
                x_ref.at[
                    chip * 2 * BLOCK : (chip + 1) * 2 * BLOCK,
                    start + first : start + first + size,
                ],
                sems.at[at, chip],
            )
            for chip, block in enumerate(blocks)
        ]
        for at, (first, size) in enumerate(((0, cut), (cut, width - cut)))
    ]


def pre_shift(x_ref, x3_ref, first, size):
    for s in range(REACH):
        wide = x_ref[s * C : (s + 1) * C, first : first + size + 2 * PAD]
        for e in range(3):
            start = PAD + e - 1
            row = (3 * s + e) * C
            x3_ref[row : row + C, :] = wide[:, start : start + size]


def convolve(matrix_ref, x_ref, x3_ref, p3_ref, width, ready, finish):
    size = width // 2
    for tile in range(2):
        first = tile * size
        wait_for(ready[tile])
        pre_shift(x_ref, x3_ref.at[tile], first, size)
        for b in range(2):
            p3_ref[b * OUT : (b + 1) * OUT, first + PAD : first + PAD + size] = jnp.dot(
                matrix_ref[b * OUT : (b + 1) * OUT, :],
                x3_ref[tile, b * STEP : b * STEP + DEEP, :],
                preferred_element_type=jnp.float32,
            )
        finish(0 if tile == 0 else size - PAD, width if tile == 1 else size - PAD)


def post_shift(p3_ref, b, first, last):
    base = b * OUT
    total = p3_ref[base + BLOCK : base + 2 * BLOCK, first + PAD : last + PAD]
    for f in (0, 2):
        wide = p3_ref[base + f * BLOCK : base + (f + 1) * BLOCK, first : last + 2 * PAD]
        start = PAD + 3 * (f - 1)
        total = total + wide[:, start : start + last - first]
    return total


def forward_kernel(
    matrix_ref, table_ref, low, own, high, cot_own, cot_mate, out_ref, x_ref, x3_ref, p3_ref, cot_ref, sems, cot_sems
):
    width = own.shape[1]
    copies = chip_copies((low, own, high), width, x_ref, sems, PAD)
    cot_copies = window_copies(cot_own, cot_mate, cot_ref, cot_sems)
    out_ref[:C, width:] = table_ref[...]
    out_ref[C:, width:] = jnp.zeros((2 * BLOCK - C, LANES), out_ref.dtype)
    for copy in copies[0] + cot_copies + copies[1]:
        copy.start()

    def finish(first, last):
        if first == 0:
            wait_for(cot_copies)
        for b in range(2):
            rows = slice(b * BLOCK, (b + 1) * BLOCK)
            total = post_shift(p3_ref, b, first, last)
            cot = cot_ref[rows, first:last].astype(jnp.float32)
            sg = jax.nn.sigmoid(total)
            total = cot * sg * (1.0 + total * (1.0 - sg))
            out_ref[rows, first:last] = total.astype(out_ref.dtype)

    convolve(matrix_ref, x_ref, x3_ref, p3_ref, width, copies, finish)


def conv_scratch(width):
    return [
        pltpu.VMEM((REACH * C, width + 2 * PAD), jnp.bfloat16),
        pltpu.VMEM((2, 3 * REACH * C, width // 2), jnp.bfloat16),
        pltpu.VMEM((2 * OUT, width + 2 * PAD), jnp.float32),
    ]


def work(width, arrays):
    return pl.CostEstimate(
        flops=4 * OUT * DEEP * width,
        bytes_accessed=arrays * 2 * BLOCK * width * 2,
        transcendentals=0,
    )


def forward(matrix, chip_table, blocks, cots):
    width = blocks[0].shape[1]
    return pl.pallas_call(
        forward_kernel,
        out_shape=jax.ShapeDtypeStruct((2 * BLOCK, width + LANES), jnp.bfloat16),
        in_specs=[LOCAL] * 2 + [ANY] * 5,
        out_specs=LOCAL,
        scratch_shapes=conv_scratch(width)
        + [
            pltpu.VMEM((2 * BLOCK, width), jnp.bfloat16),
            pltpu.SemaphoreType.DMA((2, 3)),
            pltpu.SemaphoreType.DMA((2, 3)),
        ],
        compiler_params=pltpu.CompilerParams(vmem_limit_bytes=VMEM),
        cost_estimate=work(width, 5),
        name="forward_conv",
    )(matrix, chip_table, *blocks, *cots)


def input_filter(tables, weight_ref, matrix_ref, weight_wide, table_wide):
    weight_wide[...] = jnp.dot(
        weight_ref[...], spread_matrix("weight", (C, DEEP)), preferred_element_type=jnp.float32
    )
    row = lax.broadcasted_iota(jnp.int32, (3 * LANES, DEEP), 0)
    group = lax.broadcasted_iota(jnp.int32, (1, DEEP), 1) // C
    source = (group * 171) >> 9
    e = group - 3 * source
    for b in range(2):
        for q in range(OWN):
            whole = source + OWN * b
            tap = TAPS - 1 - source + q
            inside = jnp.logical_and(tap >= 0, tap < TAPS)
            wanted = (whole >> 2) * LANES + (whole & 3) * 3 * TAPS + 3 * tap + e
            wanted = jnp.where(inside, wanted, -1)
            picks = jnp.where(row == wanted, 1.0, 0.0).astype(jnp.bfloat16)
            table_wide[...] = jnp.dot(tables, picks, preferred_element_type=jnp.float32)
            for f in range(3):
                total = jnp.zeros((C, DEEP), jnp.float32)
                for k in range(K):
                    at = f * K + k
                    total = (
                        total
                        + table_wide[at : at + 1, :] * weight_wide[k * C : (k + 1) * C, :]
                    )
                first = b * OUT + f * BLOCK + q * C
                matrix_ref[first : first + C, :] = total.astype(jnp.bfloat16)


def backward_kernel(
    weight_ref, low, own, high, whole, give,
    x_ref, x3_ref, p3_ref, o_ref, t_ref, matrix_ref, weight_wide, table_wide,
    sems, table_sems, out_sems,
):
    width = own.shape[1] - LANES
    half = width - 2 * PAD
    table_copies = [
        pltpu.make_async_copy(
            block.at[0:C, width : width + LANES],
            t_ref.at[:, chip * LANES : (chip + 1) * LANES],
            table_sems.at[chip],
        )
        for chip, block in enumerate((low, own, high))
    ]
    copies = chip_copies((low, own, high), width, x_ref, sems, PAD)
    for copy in table_copies + copies[0] + copies[1]:
        copy.start()
    wait_for(table_copies)
    input_filter(t_ref[...], weight_ref, matrix_ref, weight_wide, table_wide)

    def finish(first, last):
        first, last = max(first, PAD), min(last, width - PAD)
        for b in range(2):
            total = post_shift(p3_ref, b, first, last)
            o_ref[b * BLOCK : (b + 1) * BLOCK, first - PAD : last - PAD] = total.astype(
                o_ref.dtype
            )

    convolve(matrix_ref, x_ref, x3_ref, p3_ref, width, copies, finish)
    mine = pl.multiple_of(core() * BLOCK, BLOCK)
    other = pl.multiple_of((1 - core()) * BLOCK, BLOCK)
    column = pl.multiple_of(core() * half, PAD)
    sends = [
        pltpu.make_async_copy(o_ref.at[pl.ds(other, BLOCK), :], give, out_sems.at[0]),
        pltpu.make_async_copy(
            o_ref.at[pl.ds(mine, BLOCK), :], whole.at[:, pl.ds(column, half)], out_sems.at[1]
        ),
    ]
    for copy in sends:
        copy.start()
    wait_for(sends)


def backward(weights, low, own, high):
    width = own.shape[1] - LANES
    half = width - 2 * PAD
    return pl.pallas_call(
        backward_kernel,
        out_shape=(
            jax.ShapeDtypeStruct((BLOCK, 2 * half), jnp.bfloat16),
            jax.ShapeDtypeStruct((BLOCK, half), jnp.bfloat16),
        ),
        in_specs=[LOCAL] + [ANY] * 3,
        out_specs=(ANY, ANY),
        scratch_shapes=conv_scratch(width)
        + [
            pltpu.VMEM((2 * BLOCK, half), jnp.bfloat16),
            pltpu.VMEM((C, 3 * LANES), jnp.bfloat16),
            pltpu.VMEM((2 * OUT, DEEP), jnp.bfloat16),
            pltpu.VMEM((K * C, DEEP), jnp.float32),
            pltpu.VMEM((C, DEEP), jnp.float32),
            pltpu.SemaphoreType.DMA((2, 3)),
            pltpu.SemaphoreType.DMA((3,)),
            pltpu.SemaphoreType.DMA((2,)),
        ],
        compiler_params=pltpu.CompilerParams(vmem_limit_bytes=VMEM + 2 * 1024 * 1024),
        cost_estimate=work(width, 4),
        name="input_conv",
    )(weights, low, own, high)


def weight_kernel(
    scale, low, own, high, delta, table_ref, out_ref,
    x_ref, x3_ref, d_ref, d3_ref, g_ref, w_ref, table_wide, sems, dsem,
):
    width = delta.shape[1] - LANES
    size = width // 2 - PAD
    copies = chip_copies((low, own, high), width, x_ref, sems, 0)
    copies[0].append(pltpu.make_async_copy(delta.at[:, 0:width], d_ref, dsem))
    for copy in copies[0] + copies[1]:
        copy.start()
    table_wide[...] = jnp.dot(
        table_ref[...],
        spread_matrix("table", (3 * SPAN, DEEP)),
        preferred_element_type=jnp.float32,
    )
    for tile in range(2):
        first = tile * size
        wait_for(copies[tile])
        pre_shift(x_ref, x3_ref.at[tile], first, size)
        wide = d_ref[:, first : first + size + 2 * PAD]
        for f in range(3):
            start = PAD - 3 * (f - 1)
            for b in range(2):
                row = b * OUT + f * BLOCK
                d3_ref[tile, row : row + BLOCK, :] = wide[
                    b * BLOCK : (b + 1) * BLOCK, start : start + size
                ]
        for b in range(2):
            rows = slice(b * OUT, (b + 1) * OUT)
            product = lax.dot_general(
                d3_ref[tile, rows, :],
                x3_ref[tile, b * STEP : b * STEP + DEEP, :],
                (((1,), (1,)), ((), ())),
                preferred_element_type=jnp.float32,
            )
            if tile == 0:
                g_ref[rows, :] = product
            else:
                g_ref[rows, :] += product

    whole = DEEP // LANES
    for k in range(K):
        total = jnp.zeros((C, DEEP), jnp.float32)
        for group in range(3 * CHIP):
            at = group * K + k
            total = total + table_wide[at : at + 1, :] * g_ref[group * C : (group + 1) * C, :]
        narrow = jnp.concatenate(
            [total[:, whole * LANES :], jnp.zeros((C, (whole + 1) * LANES - DEEP), jnp.float32)],
            axis=1,
        )
        for part in range(whole):
            narrow = narrow + total[:, part * LANES : (part + 1) * LANES]
        w_ref[k * C : (k + 1) * C, :] = narrow
    row = lax.broadcasted_iota(jnp.int32, (LANES, LANES), 0)
    lane = lax.broadcasted_iota(jnp.int32, (LANES, LANES), 1)
    result = jnp.zeros((K * C // 4, LANES), jnp.float32)
    for c in range(4):
        fold = jnp.where(lane == c * C + row % C, 1.0, 0.0)
        result = result + jnp.dot(
            w_ref[pl.ds(c, K * C // 4, stride=4), :],
            fold,
            preferred_element_type=jnp.float32,
            precision=lax.Precision.HIGHEST,
        )
    out_ref[...] = result * scale


def weight_part(blocks, delta, table, scale):
    width = delta.shape[1] - LANES
    return pl.pallas_call(
        functools.partial(weight_kernel, scale),
        out_shape=jax.ShapeDtypeStruct((K * C // 4, LANES), jnp.float32),
        in_specs=[ANY] * 4 + [LOCAL],
        out_specs=LOCAL,
        scratch_shapes=[
            pltpu.VMEM((REACH * C, width), jnp.bfloat16),
            pltpu.VMEM((2, 3 * REACH * C, width // 2 - PAD), jnp.bfloat16),
            pltpu.VMEM((2 * BLOCK, width), jnp.bfloat16),
            pltpu.VMEM((2, 2 * OUT, width // 2 - PAD), jnp.bfloat16),
            pltpu.VMEM((2 * OUT, DEEP), jnp.float32),
            pltpu.VMEM((K * C, LANES), jnp.float32),
            pltpu.VMEM((3 * CHIP * K, DEEP), jnp.float32),
            pltpu.SemaphoreType.DMA((2, 3)),
            pltpu.SemaphoreType.DMA,
        ],
        compiler_params=pltpu.CompilerParams(vmem_limit_bytes=VMEM),
        cost_estimate=work(width, 4),
        name="weight_part",
    )(*blocks, delta, table)


def moved(array, by):
    peers = lax.axis_size("lat")
    return lax.ppermute(
        array, "lat", [(i, i + by) for i in range(peers) if 0 <= i + by < peers]
    )


def swapped(array, bit=1):
    return lax.ppermute(array, "lat", [(i, i ^ bit) for i in range(lax.axis_size("lat"))])


def summed(part, bits):
    if len(bits) == 1:
        return part + swapped(part, bits[0])
    one, two = bits
    others = [swapped(part, bit) for bit in (one, two, one + two)]
    return (part + others[0]) + (others[1] + others[2])


def as_table(padded):
    parts = padded.reshape(2, OWN, SPAN, 3, 3, K)
    return jnp.transpose(parts, (0, 3, 1, 5, 2, 4)).reshape(3 * CHIP * K, 3 * SPAN)


def forward_table(pair):
    rows = pair.reshape(2, OWN, TAPS, TAPS, K)
    return as_table(
        jnp.stack(
            [
                jnp.pad(rows[:, r], ((0, 0), (r, SPAN - TAPS - r), (0, 0), (0, 0)))
                for r in range(OWN)
            ],
            axis=1,
        )
    )


def sent_table(pair):
    parts = pair[:, :, ::-1].reshape(CHIP, TAPS, 3, 3, K)
    flat = jnp.transpose(parts, (2, 4, 0, 1, 3)).reshape(3 * K, 3 * CHIP * TAPS)
    return jnp.pad(flat, ((0, C - 3 * K), (0, LANES - 3 * CHIP * TAPS)))


def body(features, cotangent, basis_table, lon_reach, weights):
    longitude = features.shape[2]
    peers = lax.axis_size("lat")

    own = features.reshape(BLOCK, longitude)
    cot_own = cotangent.reshape(BLOCK, longitude)
    own_mate = swapped(own)

    offsets = jnp.arange(TAPS, dtype=jnp.int32) - RAD
    inside = jnp.abs(offsets)[None, None, :] <= lon_reach[:, :, None]
    masked = jnp.where(inside[..., None], basis_table, jnp.zeros_like(basis_table))
    mate = swapped(masked)
    pair = jnp.where(
        core() == 0, jnp.concatenate([masked, mate]), jnp.concatenate([mate, masked])
    )
    window = chip_window(own, own_mate)
    low, high = moved(window, 2), moved(window, -2)
    cot_mate = swapped(cot_own)

    table = forward_table(pair)
    matrix = make_filter(table, weights.reshape(K * C, C))
    blocks, matrix, cot_mate = lax.optimization_barrier(
        ((low, window, high), matrix, cot_mate)
    )
    delta = forward(matrix, sent_table(pair), blocks, (cot_own, cot_mate))

    low, high = moved(delta, 2), moved(delta, -2)
    scale = 1.0 / math.sqrt(peers * OWN * longitude)
    total = weight_part(blocks, delta, table, scale)
    for bits in ((1,), (8, 16)):
        total = summed(total, bits)
    low, high, total = lax.optimization_barrier((low, high, total))
    turned = jnp.transpose(weights, (0, 2, 1)).reshape(K * C, C)
    whole, give = backward(turned, low, delta, high)
    got = swapped(give)
    for bits in ((32, 64), (2, 4)):
        total = summed(total, bits)
    grad_input = join(got, whole)
    return grad_input.reshape(OWN, C, longitude), total.reshape(K, C, C)


def solution(mesh):
    in_specs = (
        P("lat", None, None),
        P("lat", None, None),
        P("lat", None, None, None),
        P("lat", None),
        P(),
    )
    out_specs = (P("lat", None, None), P())
    return jax.shard_map(body, mesh=mesh, in_specs=in_specs, out_specs=out_specs, check_vma=False)
```

```python
import functools
import math

import jax
import jax.numpy as jnp
from jax import lax
from jax.experimental import pallas as pl
from jax.experimental.pallas import tpu as pltpu
from jax.sharding import PartitionSpec as P

C = 32
K = 9
RAD = 4
TAPS = 9
OWN = 2
SPAN = OWN + 2 * RAD
CHIP = 2 * OWN
REACH = 3 * CHIP
BLOCK = OWN * C
STEP = 3 * BLOCK
DEEP = 3 * SPAN * C
OUT = 3 * BLOCK
PAD = 128
LANES = 128
VMEM = 24 * 1024 * 1024
SMALL = 8 * 1024 * 1024
LARGE = 58 * 1024 * 1024
ANY = pl.BlockSpec(memory_space=pl.ANY)
LOCAL = pl.BlockSpec(memory_space=pltpu.VMEM)


def core():
    return lax.rem(lax.axis_index("lat"), 2)


def spread_matrix(kind, shape):
    row = lax.broadcasted_iota(jnp.int32, shape, 0)
    lane = lax.broadcasted_iota(jnp.int32, shape, 1)
    hit = (lane // C == row) if kind == "table" else (lane % C == row)
    return jnp.where(hit, 1.0, 0.0).astype(jnp.bfloat16)


def filter_kernel(table_ref, weight_ref, out_ref, table_wide, weight_wide):
    table_wide[...] = jnp.dot(
        table_ref[...],
        spread_matrix("table", (3 * SPAN, DEEP)),
        preferred_element_type=jnp.float32,
    )
    weight_wide[...] = jnp.dot(
        weight_ref[...], spread_matrix("weight", (C, DEEP)), preferred_element_type=jnp.float32
    )
    for group in range(3 * CHIP):
        total = jnp.zeros((C, DEEP), jnp.float32)
        for k in range(K):
            at = group * K + k
            total = total + table_wide[at : at + 1, :] * weight_wide[k * C : (k + 1) * C, :]
        out_ref[group * C : (group + 1) * C, :] = total.astype(jnp.bfloat16)


def make_filter(table, weights):
    return pl.pallas_call(
        filter_kernel,
        out_shape=jax.ShapeDtypeStruct((2 * OUT, DEEP), jnp.bfloat16),
        in_specs=[LOCAL] * 2,
        out_specs=LOCAL,
        scratch_shapes=[
            pltpu.VMEM((3 * CHIP * K, DEEP), jnp.float32),
            pltpu.VMEM((K * C, DEEP), jnp.float32),
        ],
        compiler_params=pltpu.CompilerParams(vmem_limit_bytes=SMALL),
        name="make_filter",
    )(table, weights)


def wait_for(copies):
    for copy in copies:
        copy.wait()


def window_copies(own, mate, target, sems):
    longitude = own.shape[1]
    half = longitude // 2
    copies = []
    for side, (whole, place) in enumerate(((own, core()), (mate, 1 - core()))):
        row = pl.multiple_of(place * BLOCK, BLOCK)
        for at, (source, start, size) in enumerate(
            (
                (core() * half, PAD, half),
                (longitude - PAD - core() * half, 0, PAD),
                (half - core() * half, PAD + half, PAD),
            )
        ):
            copies.append(
                pltpu.make_async_copy(
                    whole.at[:, pl.ds(pl.multiple_of(source, PAD), size)],
                    target.at[pl.ds(row, BLOCK), pl.ds(start, size)],
                    sems.at[side, at],
                )
            )
    return copies


def window_kernel(own, mate, out_ref, sems):
    copies = window_copies(own, mate, out_ref, sems)
    for copy in copies:
        copy.start()
    wait_for(copies)


def chip_window(own, mate):
    return pl.pallas_call(
        window_kernel,
        out_shape=jax.ShapeDtypeStruct((2 * BLOCK, own.shape[1] // 2 + 2 * PAD), own.dtype),
        in_specs=[ANY, ANY],
        out_specs=LOCAL,
        scratch_shapes=[pltpu.SemaphoreType.DMA((2, 3))],
        compiler_params=pltpu.CompilerParams(vmem_limit_bytes=SMALL),
        name="chip_window",
    )(own, mate)


def join_kernel(got, whole, out, sem):
    half = whole.shape[1] // 2
    start = pl.multiple_of((1 - core()) * half, PAD)
    copy = pltpu.make_async_copy(got, out.at[:, pl.ds(start, half)], sem)
    copy.start()
    copy.wait()


def join(got, whole):
    return pl.pallas_call(
        join_kernel,
        out_shape=jax.ShapeDtypeStruct(whole.shape, whole.dtype),
        in_specs=[LOCAL, ANY],
        out_specs=ANY,
        scratch_shapes=[pltpu.SemaphoreType.DMA],
        input_output_aliases={1: 0},
        compiler_params=pltpu.CompilerParams(vmem_limit_bytes=VMEM),
        name="join",
    )(got, whole)


def in_parts(width):
    cut = width // 2 + PAD
    return ((0, cut), (cut, width - cut))


def chip_copies(blocks, width, x_ref, sems, start):
    cut = width // 2 + PAD
    return [
        [
            pltpu.make_async_copy(
                block.at[:, first : first + size],
                x_ref.at[
                    chip * 2 * BLOCK : (chip + 1) * 2 * BLOCK,
                    start + first : start + first + size,
                ],
                sems.at[at, chip],
            )
            for chip, block in enumerate(blocks)
        ]
        for at, (first, size) in enumerate(((0, cut), (cut, width - cut)))
    ]


def pre_shift(x_ref, x3_ref, first, size):
    for s in range(REACH):
        wide = x_ref[s * C : (s + 1) * C, first : first + size + 2 * PAD]
        for e in range(3):
            start = PAD + e - 1
            row = (3 * s + e) * C
            x3_ref[row : row + C, :] = wide[:, start : start + size]


def convolve(matrix_ref, x_ref, x3_ref, p3_ref, width, ready, finish):
    size = width // 2
    for tile in range(2):
        first = tile * size
        wait_for(ready[tile])
        pre_shift(x_ref, x3_ref.at[tile], first, size)
        for b in range(2):
            p3_ref[b * OUT : (b + 1) * OUT, first + PAD : first + PAD + size] = jnp.dot(
                matrix_ref[b * OUT : (b + 1) * OUT, :],
                x3_ref[tile, b * STEP : b * STEP + DEEP, :],
                preferred_element_type=jnp.float32,
            )
        finish(0 if tile == 0 else size - PAD, width if tile == 1 else size - PAD)


def post_shift(p3_ref, b, first, last):
    base = b * OUT
    total = p3_ref[base + BLOCK : base + 2 * BLOCK, first + PAD : last + PAD]
    for f in (0, 2):
        wide = p3_ref[base + f * BLOCK : base + (f + 1) * BLOCK, first : last + 2 * PAD]
        start = PAD + 3 * (f - 1)
        total = total + wide[:, start : start + last - first]
    return total


def forward_kernel(
    matrix_ref, table_ref, low, own, high, cot_own, cot_mate, out_ref, x_ref,
    x3_ref, p3_ref, cot_ref, sems, cot_sems,
):
    width = own.shape[1]
    copies = chip_copies((low, own, high), width, x_ref, sems, PAD)
    cot_copies = window_copies(cot_own, cot_mate, cot_ref, cot_sems)
    out_ref[:C, width:] = table_ref[...]
    out_ref[C:, width:] = jnp.zeros((2 * BLOCK - C, LANES), out_ref.dtype)
    for copy in copies[0] + cot_copies + copies[1]:
        copy.start()

    def finish(first, last):
        if first == 0:
            wait_for(cot_copies)
        for b in range(2):
            rows = slice(b * BLOCK, (b + 1) * BLOCK)
            total = post_shift(p3_ref, b, first, last)
            cot = cot_ref[rows, first:last].astype(jnp.float32)
            sg = jax.nn.sigmoid(total)
            total = cot * sg * (1.0 + total * (1.0 - sg))
            out_ref[rows, first:last] = total.astype(out_ref.dtype)

    convolve(matrix_ref, x_ref, x3_ref, p3_ref, width, copies, finish)


def conv_scratch(width):
    return [
        pltpu.VMEM((REACH * C, width + 2 * PAD), jnp.bfloat16),
        pltpu.VMEM((2, 3 * REACH * C, width // 2), jnp.bfloat16),
        pltpu.VMEM((2 * OUT, width + 2 * PAD), jnp.float32),
    ]


def work(width, arrays):
    return pl.CostEstimate(
        flops=4 * OUT * DEEP * width,
        bytes_accessed=arrays * 2 * BLOCK * width * 2,
        transcendentals=0,
    )


def forward(matrix, chip_table, blocks, cots):
    width = blocks[0].shape[1]
    return pl.pallas_call(
        forward_kernel,
        out_shape=(
            jax.ShapeDtypeStruct((2 * BLOCK, width + LANES), jnp.bfloat16),
            jax.ShapeDtypeStruct((REACH * C, width + 2 * PAD), jnp.bfloat16),
        ),
        in_specs=[LOCAL] * 2 + [ANY] * 5,
        out_specs=(LOCAL, LOCAL),
        scratch_shapes=conv_scratch(width)[1:]
        + [
            pltpu.VMEM((2 * BLOCK, width), jnp.bfloat16),
            pltpu.SemaphoreType.DMA((2, 3)),
            pltpu.SemaphoreType.DMA((2, 3)),
        ],
        compiler_params=pltpu.CompilerParams(vmem_limit_bytes=VMEM - 4 * 1024 * 1024),
        cost_estimate=work(width, 5),
        name="forward_conv",
    )(matrix, chip_table, *blocks, *cots)


def input_filter(tables, weight_ref, matrix_ref, weight_wide, table_wide):
    weight_wide[...] = jnp.dot(
        weight_ref[...], spread_matrix("weight", (C, DEEP)), preferred_element_type=jnp.float32
    )
    row = lax.broadcasted_iota(jnp.int32, (3 * LANES, DEEP), 0)
    group = lax.broadcasted_iota(jnp.int32, (1, DEEP), 1) // C
    source = (group * 171) >> 9
    e = group - 3 * source
    for b in range(2):
        for q in range(OWN):
            whole = source + OWN * b
            tap = TAPS - 1 - source + q
            inside = jnp.logical_and(tap >= 0, tap < TAPS)
            wanted = (whole >> 2) * LANES + (whole & 3) * 3 * TAPS + 3 * tap + e
            wanted = jnp.where(inside, wanted, -1)
            picks = jnp.where(row == wanted, 1.0, 0.0).astype(jnp.bfloat16)
            table_wide[...] = jnp.dot(tables, picks, preferred_element_type=jnp.float32)
            for f in range(3):
                total = jnp.zeros((C, DEEP), jnp.float32)
                for k in range(K):
                    at = f * K + k
                    total = (
                        total
                        + table_wide[at : at + 1, :] * weight_wide[k * C : (k + 1) * C, :]
                    )
                first = b * OUT + f * BLOCK + q * C
                matrix_ref[first : first + C, :] = total.astype(jnp.bfloat16)


def backward_kernel(
    weight_ref, low, own, high, whole, give,
    x_ref, x3_ref, p3_ref, o_ref, t_ref, matrix_ref, weight_wide, table_wide,
    sems, table_sems, out_sems,
):
    width = own.shape[1] - LANES
    half = width - 2 * PAD
    table_copies = [
        pltpu.make_async_copy(
            block.at[0:C, width : width + LANES],
            t_ref.at[:, chip * LANES : (chip + 1) * LANES],
            table_sems.at[chip],
        )
        for chip, block in enumerate((low, own, high))
    ]
    copies = chip_copies((low, own, high), width, x_ref, sems, PAD)
    for copy in table_copies + copies[0] + copies[1]:
        copy.start()
    wait_for(table_copies)
    input_filter(t_ref[...], weight_ref, matrix_ref, weight_wide, table_wide)

    def finish(first, last):
        first, last = max(first, PAD), min(last, width - PAD)
        for b in range(2):
            total = post_shift(p3_ref, b, first, last)
            o_ref[b * BLOCK : (b + 1) * BLOCK, first - PAD : last - PAD] = total.astype(
                o_ref.dtype
            )

    convolve(matrix_ref, x_ref, x3_ref, p3_ref, width, copies, finish)
    mine = pl.multiple_of(core() * BLOCK, BLOCK)
    other = pl.multiple_of((1 - core()) * BLOCK, BLOCK)
    column = pl.multiple_of(core() * half, PAD)
    sends = [
        pltpu.make_async_copy(o_ref.at[pl.ds(other, BLOCK), :], give, out_sems.at[0]),
        pltpu.make_async_copy(
            o_ref.at[pl.ds(mine, BLOCK), :], whole.at[:, pl.ds(column, half)], out_sems.at[1]
        ),
    ]
    for copy in sends:
        copy.start()
    wait_for(sends)


def backward(weights, low, own, high):
    width = own.shape[1] - LANES
    half = width - 2 * PAD
    return pl.pallas_call(
        backward_kernel,
        out_shape=(
            jax.ShapeDtypeStruct((BLOCK, 2 * half), jnp.bfloat16),
            jax.ShapeDtypeStruct((BLOCK, half), jnp.bfloat16),
        ),
        in_specs=[LOCAL] + [ANY] * 3,
        out_specs=(ANY, ANY),
        scratch_shapes=conv_scratch(width)
        + [
            pltpu.VMEM((2 * BLOCK, half), jnp.bfloat16),
            pltpu.VMEM((C, 3 * LANES), jnp.bfloat16),
            pltpu.VMEM((2 * OUT, DEEP), jnp.bfloat16),
            pltpu.VMEM((K * C, DEEP), jnp.float32),
            pltpu.VMEM((C, DEEP), jnp.float32),
            pltpu.SemaphoreType.DMA((2, 3)),
            pltpu.SemaphoreType.DMA((3,)),
            pltpu.SemaphoreType.DMA((2,)),
        ],
        compiler_params=pltpu.CompilerParams(vmem_limit_bytes=VMEM + 2 * 1024 * 1024),
        cost_estimate=work(width, 4),
        name="input_conv",
    )(weights, low, own, high)


def weight_kernel(
    scale, x_ref, d_ref, table_ref, out_ref, x3_ref, d3_ref, g_ref, w_ref, table_wide
):
    width = d_ref.shape[1] - LANES
    size = width // 2 - PAD
    table_wide[...] = jnp.dot(
        table_ref[...],
        spread_matrix("table", (3 * SPAN, DEEP)),
        preferred_element_type=jnp.float32,
    )
    for tile in range(2):
        first = tile * size
        pre_shift(x_ref, x3_ref.at[tile], first + PAD, size)
        wide = d_ref[:, first : first + size + 2 * PAD]
        for f in range(3):
            start = PAD - 3 * (f - 1)
            for b in range(2):
                row = b * OUT + f * BLOCK
                d3_ref[tile, row : row + BLOCK, :] = wide[
                    b * BLOCK : (b + 1) * BLOCK, start : start + size
                ]
        for b in range(2):
            rows = slice(b * OUT, (b + 1) * OUT)
            product = lax.dot_general(
                d3_ref[tile, rows, :],
                x3_ref[tile, b * STEP : b * STEP + DEEP, :],
                (((1,), (1,)), ((), ())),
                preferred_element_type=jnp.float32,
            )
            if tile == 0:
                g_ref[rows, :] = product
            else:
                g_ref[rows, :] += product

    whole = DEEP // LANES
    for k in range(K):
        total = jnp.zeros((C, DEEP), jnp.float32)
        for group in range(3 * CHIP):
            at = group * K + k
            total = total + table_wide[at : at + 1, :] * g_ref[group * C : (group + 1) * C, :]
        narrow = jnp.concatenate(
            [total[:, whole * LANES :], jnp.zeros((C, (whole + 1) * LANES - DEEP), jnp.float32)],
            axis=1,
        )
        for part in range(whole):
            narrow = narrow + total[:, part * LANES : (part + 1) * LANES]
        w_ref[k * C : (k + 1) * C, :] = narrow
    row = lax.broadcasted_iota(jnp.int32, (LANES, LANES), 0)
    lane = lax.broadcasted_iota(jnp.int32, (LANES, LANES), 1)
    result = jnp.zeros((K * C // 4, LANES), jnp.float32)
    for c in range(4):
        fold = jnp.where(lane == c * C + row % C, 1.0, 0.0)
        result = result + jnp.dot(
            w_ref[pl.ds(c, K * C // 4, stride=4), :],
            fold,
            preferred_element_type=jnp.float32,
            precision=lax.Precision.HIGHEST,
        )
    out_ref[...] = result * scale


def weight_part(joined, delta, table, scale):
    width = delta.shape[1] - LANES
    return pl.pallas_call(
        functools.partial(weight_kernel, scale),
        out_shape=jax.ShapeDtypeStruct((K * C // 4, LANES), jnp.float32),
        in_specs=[LOCAL] * 3,
        out_specs=LOCAL,
        scratch_shapes=[
            pltpu.VMEM((2, 3 * REACH * C, width // 2 - PAD), jnp.bfloat16),
            pltpu.VMEM((2, 2 * OUT, width // 2 - PAD), jnp.bfloat16),
            pltpu.VMEM((2 * OUT, DEEP), jnp.float32),
            pltpu.VMEM((K * C, LANES), jnp.float32),
            pltpu.VMEM((3 * CHIP * K, DEEP), jnp.float32),
        ],
        compiler_params=pltpu.CompilerParams(vmem_limit_bytes=VMEM - 6 * 1024 * 1024),
        cost_estimate=work(width, 4),
        name="weight_part",
    )(joined, delta, table)


def moved(array, by):
    peers = lax.axis_size("lat")
    return lax.ppermute(
        array, "lat", [(i, i + by) for i in range(peers) if 0 <= i + by < peers]
    )


def swapped(array, bit=1):
    return lax.ppermute(array, "lat", [(i, i ^ bit) for i in range(lax.axis_size("lat"))])


def summed(part, bits):
    if len(bits) == 1:
        return part + swapped(part, bits[0])
    one, two = bits
    others = [swapped(part, bit) for bit in (one, two, one + two)]
    return (part + others[0]) + (others[1] + others[2])


def as_table(padded):
    parts = padded.reshape(2, OWN, SPAN, 3, 3, K)
    return jnp.transpose(parts, (0, 3, 1, 5, 2, 4)).reshape(3 * CHIP * K, 3 * SPAN)


def forward_table(pair):
    rows = pair.reshape(2, OWN, TAPS, TAPS, K)
    return as_table(
        jnp.stack(
            [
                jnp.pad(rows[:, r], ((0, 0), (r, SPAN - TAPS - r), (0, 0), (0, 0)))
                for r in range(OWN)
            ],
            axis=1,
        )
    )


def sent_table(pair):
    parts = pair[:, :, ::-1].reshape(CHIP, TAPS, 3, 3, K)
    flat = jnp.transpose(parts, (2, 4, 0, 1, 3)).reshape(3 * K, 3 * CHIP * TAPS)
    return jnp.pad(flat, ((0, C - 3 * K), (0, LANES - 3 * CHIP * TAPS)))


def body(features, cotangent, basis_table, lon_reach, weights):
    longitude = features.shape[2]
    peers = lax.axis_size("lat")

    own = features.reshape(BLOCK, longitude)
    cot_own = cotangent.reshape(BLOCK, longitude)
    own_mate = swapped(own)

    offsets = jnp.arange(TAPS, dtype=jnp.int32) - RAD
    inside = jnp.abs(offsets)[None, None, :] <= lon_reach[:, :, None]
    masked = jnp.where(inside[..., None], basis_table, jnp.zeros_like(basis_table))
    mate = swapped(masked)
    pair = jnp.where(
        core() == 0, jnp.concatenate([masked, mate]), jnp.concatenate([mate, masked])
    )
    window = chip_window(own, own_mate)
    low, high = moved(window, 2), moved(window, -2)
    cot_mate = swapped(cot_own)

    table = forward_table(pair)
    matrix = make_filter(table, weights.reshape(K * C, C))
    delta, joined = forward(
        matrix, sent_table(pair), (low, window, high), (cot_own, cot_mate)
    )

    low, high = moved(delta, 2), moved(delta, -2)
    scale = 1.0 / math.sqrt(peers * OWN * longitude)
    total = weight_part(joined, delta, table, scale)
    for bits in ((1,), (32, 64)):
        total = summed(total, bits)
    low, high, total = lax.optimization_barrier((low, high, total))
    turned = jnp.transpose(weights, (0, 2, 1)).reshape(K * C, C)
    whole, give = backward(turned, low, delta, high)
    got = swapped(give)
    for bits in ((8, 16), (2, 4)):
        total = summed(total, bits)
    grad_input = join(got, whole)
    return grad_input.reshape(OWN, C, longitude), total.reshape(K, C, C)


def solution(mesh):
    in_specs = (
        P("lat", None, None),
        P("lat", None, None),
        P("lat", None, None, None),
        P("lat", None),
        P(),
    )
    out_specs = (P("lat", None, None), P())
    return jax.shard_map(body, mesh=mesh, in_specs=in_specs, out_specs=out_specs, check_vma=False)
```

```python
import functools
import math

import jax
import jax.numpy as jnp
from jax import lax
from jax.experimental import pallas as pl
from jax.experimental.pallas import tpu as pltpu
from jax.sharding import PartitionSpec as P

C = 32
K = 9
RAD = 4
TAPS = 9
OWN = 2
SPAN = OWN + 2 * RAD
CHIP = 2 * OWN
REACH = 3 * CHIP
BLOCK = OWN * C
STEP = 3 * BLOCK
DEEP = 3 * SPAN * C
OUT = 3 * BLOCK
PAD = 128
LANES = 128
VMEM = 26 * 1024 * 1024
SMALL = VMEM
LARGE = 58 * 1024 * 1024
ANY = pl.BlockSpec(memory_space=pl.ANY)
LOCAL = pl.BlockSpec(memory_space=pltpu.VMEM)


def core():
    return lax.rem(lax.axis_index("lat"), 2)


def spread_matrix(kind, shape):
    row = lax.broadcasted_iota(jnp.int32, shape, 0)
    lane = lax.broadcasted_iota(jnp.int32, shape, 1)
    hit = (lane // C == row) if kind == "table" else (lane % C == row)
    return jnp.where(hit, 1.0, 0.0).astype(jnp.bfloat16)


def filter_kernel(table_ref, weight_ref, out_ref, table_wide, weight_wide):
    table_wide[...] = jnp.dot(
        table_ref[...],
        spread_matrix("table", (3 * SPAN, DEEP)),
        preferred_element_type=jnp.float32,
    )
    weight_wide[...] = jnp.dot(
        weight_ref[...], spread_matrix("weight", (C, DEEP)), preferred_element_type=jnp.float32
    )
    for group in range(3 * CHIP):
        total = jnp.zeros((C, DEEP), jnp.float32)
        for k in range(K):
            at = group * K + k
            total = total + table_wide[at : at + 1, :] * weight_wide[k * C : (k + 1) * C, :]
        out_ref[group * C : (group + 1) * C, :] = total.astype(jnp.bfloat16)


def make_filter(table, weights):
    return pl.pallas_call(
        filter_kernel,
        out_shape=jax.ShapeDtypeStruct((2 * OUT, DEEP), jnp.bfloat16),
        in_specs=[LOCAL] * 2,
        out_specs=LOCAL,
        scratch_shapes=[
            pltpu.VMEM((3 * CHIP * K, DEEP), jnp.float32),
            pltpu.VMEM((K * C, DEEP), jnp.float32),
        ],
        compiler_params=pltpu.CompilerParams(vmem_limit_bytes=SMALL),
        name="make_filter",
    )(table, weights)


def wait_for(copies):
    for copy in copies:
        copy.wait()


def window_copies(own, mate, target, sems):
    longitude = own.shape[1]
    half = longitude // 2
    copies = []
    for side, (whole, place) in enumerate(((own, core()), (mate, 1 - core()))):
        row = pl.multiple_of(place * BLOCK, BLOCK)
        for at, (source, start, size) in enumerate(
            (
                (core() * half, PAD, half),
                (longitude - PAD - core() * half, 0, PAD),
                (half - core() * half, PAD + half, PAD),
            )
        ):
            copies.append(
                pltpu.make_async_copy(
                    whole.at[:, pl.ds(pl.multiple_of(source, PAD), size)],
                    target.at[pl.ds(row, BLOCK), pl.ds(start, size)],
                    sems.at[side, at],
                )
            )
    return copies


def window_pieces(whole, target, row, sems):
    longitude = whole.shape[1]
    half = longitude // 2
    return [
        pltpu.make_async_copy(
            whole.at[:, pl.ds(pl.multiple_of(source, PAD), size)],
            target.at[pl.ds(row, BLOCK), pl.ds(start, size)],
            sems.at[at],
        )
        for at, (source, start, size) in enumerate(
            (
                (core() * half, PAD, half),
                (longitude - PAD - core() * half, 0, PAD),
                (half - core() * half, PAD + half, PAD),
            )
        )
    ]


def own_kernel(own, out_ref, sems):
    copies = window_pieces(own, out_ref, 0, sems)
    for copy in copies:
        copy.start()
    wait_for(copies)


def own_window(own):
    return pl.pallas_call(
        own_kernel,
        out_shape=jax.ShapeDtypeStruct((BLOCK, own.shape[1] // 2 + 2 * PAD), own.dtype),
        in_specs=[ANY],
        out_specs=LOCAL,
        scratch_shapes=[pltpu.SemaphoreType.DMA((3,))],
        compiler_params=pltpu.CompilerParams(vmem_limit_bytes=SMALL),
        name="own_window",
    )(own)


def chip_kernel(piece, mate, out_ref, sems, piece_sem):
    row = pl.multiple_of((1 - core()) * BLOCK, BLOCK)
    copies = window_pieces(mate, out_ref, row, sems)
    own_row = pl.multiple_of(core() * BLOCK, BLOCK)
    copies.append(
        pltpu.make_async_copy(piece, out_ref.at[pl.ds(own_row, BLOCK), :], piece_sem)
    )
    for copy in copies:
        copy.start()
    wait_for(copies)


def chip_window(piece, mate):
    return pl.pallas_call(
        chip_kernel,
        out_shape=jax.ShapeDtypeStruct((2 * BLOCK, piece.shape[1]), piece.dtype),
        in_specs=[ANY, ANY],
        out_specs=LOCAL,
        scratch_shapes=[pltpu.SemaphoreType.DMA((3,)), pltpu.SemaphoreType.DMA],
        compiler_params=pltpu.CompilerParams(vmem_limit_bytes=SMALL),
        name="chip_window",
    )(piece, mate)


def join_kernel(got, whole, out, sem):
    half = whole.shape[1] // 2
    start = pl.multiple_of((1 - core()) * half, PAD)
    copy = pltpu.make_async_copy(got, out.at[:, pl.ds(start, half)], sem)
    copy.start()
    copy.wait()


def join(got, whole):
    return pl.pallas_call(
        join_kernel,
        out_shape=jax.ShapeDtypeStruct(whole.shape, whole.dtype),
        in_specs=[LOCAL, ANY],
        out_specs=ANY,
        scratch_shapes=[pltpu.SemaphoreType.DMA],
        input_output_aliases={1: 0},
        compiler_params=pltpu.CompilerParams(vmem_limit_bytes=VMEM),
        name="join",
    )(got, whole)


def in_parts(width):
    cut = width // 2 + PAD
    return ((0, cut), (cut, width - cut))


def chip_copies(blocks, width, x_ref, sems, start):
    cut = width // 2 + PAD
    return [
        [
            pltpu.make_async_copy(
                block.at[:, first : first + size],
                x_ref.at[
                    chip * 2 * BLOCK : (chip + 1) * 2 * BLOCK,
                    start + first : start + first + size,
                ],
                sems.at[at, chip],
            )
            for chip, block in enumerate(blocks)
        ]
        for at, (first, size) in enumerate(((0, cut), (cut, width - cut)))
    ]


def pre_shift(x_ref, x3_ref, first, size):
    for s in range(REACH):
        wide = x_ref[s * C : (s + 1) * C, first : first + size + 2 * PAD]
        for e in range(3):
            start = PAD + e - 1
            row = (3 * s + e) * C
            x3_ref[row : row + C, :] = wide[:, start : start + size]


def convolve(matrix_ref, x_ref, x3_ref, p3_ref, width, ready, finish):
    size = width // 2
    for tile in range(2):
        first = tile * size
        wait_for(ready[tile])
        pre_shift(x_ref, x3_ref.at[tile], first, size)
        for b in range(2):
            p3_ref[b * OUT : (b + 1) * OUT, first + PAD : first + PAD + size] = jnp.dot(
                matrix_ref[b * OUT : (b + 1) * OUT, :],
                x3_ref[tile, b * STEP : b * STEP + DEEP, :],
                preferred_element_type=jnp.float32,
            )
        finish(0 if tile == 0 else size - PAD, width if tile == 1 else size - PAD)


def post_shift(p3_ref, b, first, last):
    base = b * OUT
    total = p3_ref[base + BLOCK : base + 2 * BLOCK, first + PAD : last + PAD]
    for f in (0, 2):
        wide = p3_ref[base + f * BLOCK : base + (f + 1) * BLOCK, first : last + 2 * PAD]
        start = PAD + 3 * (f - 1)
        total = total + wide[:, start : start + last - first]
    return total


def forward_kernel(
    matrix_ref, table_ref, low, own, high, cot_own, cot_mate, out_ref, x_ref,
    x3_ref, p3_ref, cot_ref, sems, cot_sems,
):
    width = own.shape[1]
    copies = chip_copies((low, own, high), width, x_ref, sems, PAD)
    cot_copies = window_copies(cot_own, cot_mate, cot_ref, cot_sems)
    out_ref[:C, width:] = table_ref[...]
    out_ref[C:, width:] = jnp.zeros((2 * BLOCK - C, LANES), out_ref.dtype)
    for copy in copies[0] + cot_copies + copies[1]:
        copy.start()

    def finish(first, last):
        if first == 0:
            wait_for(cot_copies)
        for b in range(2):
            rows = slice(b * BLOCK, (b + 1) * BLOCK)
            total = post_shift(p3_ref, b, first, last)
            cot = cot_ref[rows, first:last].astype(jnp.float32)
            sg = jax.nn.sigmoid(total)
            total = cot * sg * (1.0 + total * (1.0 - sg))
            out_ref[rows, first:last] = total.astype(out_ref.dtype)

    convolve(matrix_ref, x_ref, x3_ref, p3_ref, width, copies, finish)


def conv_scratch(width):
    return [
        pltpu.VMEM((REACH * C, width + 2 * PAD), jnp.bfloat16),
        pltpu.VMEM((2, 3 * REACH * C, width // 2), jnp.bfloat16),
        pltpu.VMEM((2 * OUT, width + 2 * PAD), jnp.float32),
    ]


def work(width, arrays):
    return pl.CostEstimate(
        flops=4 * OUT * DEEP * width,
        bytes_accessed=arrays * 2 * BLOCK * width * 2,
        transcendentals=0,
    )


def forward(matrix, chip_table, blocks, cots):
    width = blocks[0].shape[1]
    return pl.pallas_call(
        forward_kernel,
        out_shape=(
            jax.ShapeDtypeStruct((2 * BLOCK, width + LANES), jnp.bfloat16),
            jax.ShapeDtypeStruct((REACH * C, width + 2 * PAD), jnp.bfloat16),
        ),
        in_specs=[LOCAL] * 2 + [ANY] * 5,
        out_specs=(LOCAL, LOCAL),
        scratch_shapes=conv_scratch(width)[1:]
        + [
            pltpu.VMEM((2 * BLOCK, width), jnp.bfloat16),
            pltpu.SemaphoreType.DMA((2, 3)),
            pltpu.SemaphoreType.DMA((2, 3)),
        ],
        compiler_params=pltpu.CompilerParams(vmem_limit_bytes=VMEM),
        cost_estimate=work(width, 5),
        name="forward_conv",
    )(matrix, chip_table, *blocks, *cots)


def input_filter(tables, weight_ref, matrix_ref, weight_wide, table_wide):
    weight_wide[...] = jnp.dot(
        weight_ref[...], spread_matrix("weight", (C, DEEP)), preferred_element_type=jnp.float32
    )
    row = lax.broadcasted_iota(jnp.int32, (3 * LANES, DEEP), 0)
    group = lax.broadcasted_iota(jnp.int32, (1, DEEP), 1) // C
    source = (group * 171) >> 9
    e = group - 3 * source
    for b in range(2):
        for q in range(OWN):
            whole = source + OWN * b
            tap = TAPS - 1 - source + q
            inside = jnp.logical_and(tap >= 0, tap < TAPS)
            wanted = (whole >> 2) * LANES + (whole & 3) * 3 * TAPS + 3 * tap + e
            wanted = jnp.where(inside, wanted, -1)
            picks = jnp.where(row == wanted, 1.0, 0.0).astype(jnp.bfloat16)
            table_wide[...] = jnp.dot(tables, picks, preferred_element_type=jnp.float32)
            for f in range(3):
                total = jnp.zeros((C, DEEP), jnp.float32)
                for k in range(K):
                    at = f * K + k
                    total = (
                        total
                        + table_wide[at : at + 1, :] * weight_wide[k * C : (k + 1) * C, :]
                    )
                first = b * OUT + f * BLOCK + q * C
                matrix_ref[first : first + C, :] = total.astype(jnp.bfloat16)


def backward_kernel(
    weight_ref, low, own, high, whole, give,
    x_ref, x3_ref, p3_ref, o_ref, t_ref, matrix_ref, weight_wide, table_wide,
    sems, table_sems, out_sems,
):
    width = own.shape[1] - LANES
    half = width - 2 * PAD
    table_copies = [
        pltpu.make_async_copy(
            block.at[0:C, width : width + LANES],
            t_ref.at[:, chip * LANES : (chip + 1) * LANES],
            table_sems.at[chip],
        )
        for chip, block in enumerate((low, own, high))
    ]
    copies = chip_copies((low, own, high), width, x_ref, sems, PAD)
    for copy in table_copies + copies[0] + copies[1]:
        copy.start()
    wait_for(table_copies)
    input_filter(t_ref[...], weight_ref, matrix_ref, weight_wide, table_wide)

    def finish(first, last):
        first, last = max(first, PAD), min(last, width - PAD)
        for b in range(2):
            total = post_shift(p3_ref, b, first, last)
            o_ref[b * BLOCK : (b + 1) * BLOCK, first - PAD : last - PAD] = total.astype(
                o_ref.dtype
            )

    convolve(matrix_ref, x_ref, x3_ref, p3_ref, width, copies, finish)
    mine = pl.multiple_of(core() * BLOCK, BLOCK)
    other = pl.multiple_of((1 - core()) * BLOCK, BLOCK)
    column = pl.multiple_of(core() * half, PAD)
    sends = [
        pltpu.make_async_copy(o_ref.at[pl.ds(other, BLOCK), :], give, out_sems.at[0]),
        pltpu.make_async_copy(
            o_ref.at[pl.ds(mine, BLOCK), :], whole.at[:, pl.ds(column, half)], out_sems.at[1]
        ),
    ]
    for copy in sends:
        copy.start()
    wait_for(sends)


def backward(weights, low, own, high):
    width = own.shape[1] - LANES
    half = width - 2 * PAD
    return pl.pallas_call(
        backward_kernel,
        out_shape=(
            jax.ShapeDtypeStruct((BLOCK, 2 * half), jnp.bfloat16),
            jax.ShapeDtypeStruct((BLOCK, half), jnp.bfloat16),
        ),
        in_specs=[LOCAL] + [ANY] * 3,
        out_specs=(ANY, ANY),
        scratch_shapes=conv_scratch(width)
        + [
            pltpu.VMEM((2 * BLOCK, half), jnp.bfloat16),
            pltpu.VMEM((C, 3 * LANES), jnp.bfloat16),
            pltpu.VMEM((2 * OUT, DEEP), jnp.bfloat16),
            pltpu.VMEM((K * C, DEEP), jnp.float32),
            pltpu.VMEM((C, DEEP), jnp.float32),
            pltpu.SemaphoreType.DMA((2, 3)),
            pltpu.SemaphoreType.DMA((3,)),
            pltpu.SemaphoreType.DMA((2,)),
        ],
        compiler_params=pltpu.CompilerParams(vmem_limit_bytes=VMEM),
        cost_estimate=work(width, 4),
        name="input_conv",
    )(weights, low, own, high)


def weight_kernel(
    scale, x_ref, d_ref, table_ref, out_ref, x3_ref, d3_ref, g_ref, w_ref, table_wide
):
    width = d_ref.shape[1] - LANES
    size = width // 2 - PAD
    table_wide[...] = jnp.dot(
        table_ref[...],
        spread_matrix("table", (3 * SPAN, DEEP)),
        preferred_element_type=jnp.float32,
    )
    for tile in range(2):
        first = tile * size
        pre_shift(x_ref, x3_ref.at[tile], first + PAD, size)
        wide = d_ref[:, first : first + size + 2 * PAD]
        for f in range(3):
            start = PAD - 3 * (f - 1)
            for b in range(2):
                row = b * OUT + f * BLOCK
                d3_ref[tile, row : row + BLOCK, :] = wide[
                    b * BLOCK : (b + 1) * BLOCK, start : start + size
                ]
        for b in range(2):
            rows = slice(b * OUT, (b + 1) * OUT)
            product = lax.dot_general(
                d3_ref[tile, rows, :],
                x3_ref[tile, b * STEP : b * STEP + DEEP, :],
                (((1,), (1,)), ((), ())),
                preferred_element_type=jnp.float32,
            )
            if tile == 0:
                g_ref[rows, :] = product
            else:
                g_ref[rows, :] += product

    whole = DEEP // LANES
    for k in range(K):
        total = jnp.zeros((C, DEEP), jnp.float32)
        for group in range(3 * CHIP):
            at = group * K + k
            total = total + table_wide[at : at + 1, :] * g_ref[group * C : (group + 1) * C, :]
        narrow = jnp.concatenate(
            [total[:, whole * LANES :], jnp.zeros((C, (whole + 1) * LANES - DEEP), jnp.float32)],
            axis=1,
        )
        for part in range(whole):
            narrow = narrow + total[:, part * LANES : (part + 1) * LANES]
        w_ref[k * C : (k + 1) * C, :] = narrow
    row = lax.broadcasted_iota(jnp.int32, (LANES, LANES), 0)
    lane = lax.broadcasted_iota(jnp.int32, (LANES, LANES), 1)
    result = jnp.zeros((K * C // 4, LANES), jnp.float32)
    for c in range(4):
        fold = jnp.where(lane == c * C + row % C, 1.0, 0.0)
        result = result + jnp.dot(
            w_ref[pl.ds(c, K * C // 4, stride=4), :],
            fold,
            preferred_element_type=jnp.float32,
            precision=lax.Precision.HIGHEST,
        )
    out_ref[...] = result * scale


def weight_part(joined, delta, table, scale):
    width = delta.shape[1] - LANES
    return pl.pallas_call(
        functools.partial(weight_kernel, scale),
        out_shape=jax.ShapeDtypeStruct((K * C // 4, LANES), jnp.float32),
        in_specs=[LOCAL] * 3,
        out_specs=LOCAL,
        scratch_shapes=[
            pltpu.VMEM((2, 3 * REACH * C, width // 2 - PAD), jnp.bfloat16),
            pltpu.VMEM((2, 2 * OUT, width // 2 - PAD), jnp.bfloat16),
            pltpu.VMEM((2 * OUT, DEEP), jnp.float32),
            pltpu.VMEM((K * C, LANES), jnp.float32),
            pltpu.VMEM((3 * CHIP * K, DEEP), jnp.float32),
        ],
        compiler_params=pltpu.CompilerParams(vmem_limit_bytes=VMEM),
        cost_estimate=work(width, 4),
        name="weight_part",
    )(joined, delta, table)


def moved(array, by):
    peers = lax.axis_size("lat")
    return lax.ppermute(
        array, "lat", [(i, i + by) for i in range(peers) if 0 <= i + by < peers]
    )


def swapped(array, bit=1):
    return lax.ppermute(array, "lat", [(i, i ^ bit) for i in range(lax.axis_size("lat"))])


def summed(part, bits):
    if len(bits) == 1:
        return part + swapped(part, bits[0])
    one, two = bits
    others = [swapped(part, bit) for bit in (one, two, one + two)]
    return (part + others[0]) + (others[1] + others[2])


def as_table(padded):
    parts = padded.reshape(2, OWN, SPAN, 3, 3, K)
    return jnp.transpose(parts, (0, 3, 1, 5, 2, 4)).reshape(3 * CHIP * K, 3 * SPAN)


def forward_table(pair):
    rows = pair.reshape(2, OWN, TAPS, TAPS, K)
    return as_table(
        jnp.stack(
            [
                jnp.pad(rows[:, r], ((0, 0), (r, SPAN - TAPS - r), (0, 0), (0, 0)))
                for r in range(OWN)
            ],
            axis=1,
        )
    )


def sent_table(pair):
    parts = pair[:, :, ::-1].reshape(CHIP, TAPS, 3, 3, K)
    flat = jnp.transpose(parts, (2, 4, 0, 1, 3)).reshape(3 * K, 3 * CHIP * TAPS)
    return jnp.pad(flat, ((0, C - 3 * K), (0, LANES - 3 * CHIP * TAPS)))


def body(features, cotangent, basis_table, lon_reach, weights):
    longitude = features.shape[2]
    peers = lax.axis_size("lat")

    own = features.reshape(BLOCK, longitude)
    cot_own = cotangent.reshape(BLOCK, longitude)
    own_mate = swapped(own)

    offsets = jnp.arange(TAPS, dtype=jnp.int32) - RAD
    inside = jnp.abs(offsets)[None, None, :] <= lon_reach[:, :, None]
    masked = jnp.where(inside[..., None], basis_table, jnp.zeros_like(basis_table))
    mate = swapped(masked)
    pair = jnp.where(
        core() == 0, jnp.concatenate([masked, mate]), jnp.concatenate([mate, masked])
    )
    window = chip_window(own_window(own), own_mate)
    low, high = moved(window, 2), moved(window, -2)
    cot_mate = swapped(cot_own)

    table = forward_table(pair)
    matrix = make_filter(table, weights.reshape(K * C, C))
    delta, joined = forward(
        matrix, sent_table(pair), (low, window, high), (cot_own, cot_mate)
    )

    low, high = moved(delta, 2), moved(delta, -2)
    scale = 1.0 / math.sqrt(peers * OWN * longitude)
    total = weight_part(joined, delta, table, scale)
    for bits in ((1,), (32, 64)):
        total = summed(total, bits)
    low, high, total = lax.optimization_barrier((low, high, total))
    turned = jnp.transpose(weights, (0, 2, 1)).reshape(K * C, C)
    whole, give = backward(turned, low, delta, high)
    got = swapped(give)
    for bits in ((8, 16), (2, 4)):
        total = summed(total, bits)
    grad_input = join(got, whole)
    return grad_input.reshape(OWN, C, longitude), total.reshape(K, C, C)


def solution(mesh):
    in_specs = (
        P("lat", None, None),
        P("lat", None, None),
        P("lat", None, None, None),
        P("lat", None),
        P(),
    )
    out_specs = (P("lat", None, None), P())
    return jax.shard_map(body, mesh=mesh, in_specs=in_specs, out_specs=out_specs, check_vma=False)
```

```python
import functools
import math

import jax
import jax.numpy as jnp
from jax import lax
from jax.experimental import pallas as pl
from jax.experimental.pallas import tpu as pltpu
from jax.sharding import PartitionSpec as P

C = 32
K = 9
RAD = 4
TAPS = 9
OWN = 2
SPAN = OWN + 2 * RAD
CHIP = 2 * OWN
REACH = 3 * CHIP
BLOCK = OWN * C
STEP = 3 * BLOCK
DEEP = 3 * SPAN * C
OUT = 3 * BLOCK
PAD = 128
LANES = 128
VMEM = 26 * 1024 * 1024
SMALL = VMEM
LARGE = 58 * 1024 * 1024
ANY = pl.BlockSpec(memory_space=pl.ANY)
LOCAL = pl.BlockSpec(memory_space=pltpu.VMEM)


def core():
    return lax.rem(lax.axis_index("lat"), 2)


def spread_matrix(kind, shape):
    row = lax.broadcasted_iota(jnp.int32, shape, 0)
    lane = lax.broadcasted_iota(jnp.int32, shape, 1)
    hit = (lane // C == row) if kind == "table" else (lane % C == row)
    return jnp.where(hit, 1.0, 0.0).astype(jnp.bfloat16)


def filter_kernel(table_ref, weight_ref, out_ref, table_wide, weight_wide):
    table_wide[...] = jnp.dot(
        table_ref[...],
        spread_matrix("table", (3 * SPAN, DEEP)),
        preferred_element_type=jnp.float32,
    )
    weight_wide[...] = jnp.dot(
        weight_ref[...], spread_matrix("weight", (C, DEEP)), preferred_element_type=jnp.float32
    )
    for group in range(3 * CHIP):
        total = jnp.zeros((C, DEEP), jnp.float32)
        for k in range(K):
            at = group * K + k
            total = total + table_wide[at : at + 1, :] * weight_wide[k * C : (k + 1) * C, :]
        out_ref[group * C : (group + 1) * C, :] = total.astype(jnp.bfloat16)


def make_filter(table, weights):
    return pl.pallas_call(
        filter_kernel,
        out_shape=jax.ShapeDtypeStruct((2 * OUT, DEEP), jnp.bfloat16),
        in_specs=[LOCAL] * 2,
        out_specs=LOCAL,
        scratch_shapes=[
            pltpu.VMEM((3 * CHIP * K, DEEP), jnp.float32),
            pltpu.VMEM((K * C, DEEP), jnp.float32),
        ],
        compiler_params=pltpu.CompilerParams(vmem_limit_bytes=SMALL),
        name="make_filter",
    )(table, weights)


def wait_for(copies):
    for copy in copies:
        copy.wait()


def window_copies(own, mate, target, sems):
    longitude = own.shape[1]
    half = longitude // 2
    copies = []
    for side, (whole, place) in enumerate(((own, core()), (mate, 1 - core()))):
        row = pl.multiple_of(place * BLOCK, BLOCK)
        for at, (source, start, size) in enumerate(
            (
                (core() * half, PAD, half),
                (longitude - PAD - core() * half, 0, PAD),
                (half - core() * half, PAD + half, PAD),
            )
        ):
            copies.append(
                pltpu.make_async_copy(
                    whole.at[:, pl.ds(pl.multiple_of(source, PAD), size)],
                    target.at[pl.ds(row, BLOCK), pl.ds(start, size)],
                    sems.at[side, at],
                )
            )
    return copies


def window_pieces(whole, target, row, sems):
    longitude = whole.shape[1]
    half = longitude // 2
    return [
        pltpu.make_async_copy(
            whole.at[:, pl.ds(pl.multiple_of(source, PAD), size)],
            target.at[pl.ds(row, BLOCK), pl.ds(start, size)],
            sems.at[at],
        )
        for at, (source, start, size) in enumerate(
            (
                (core() * half, PAD, half),
                (longitude - PAD - core() * half, 0, PAD),
                (half - core() * half, PAD + half, PAD),
            )
        )
    ]


def own_kernel(own, out_ref, sems):
    copies = window_pieces(own, out_ref, 0, sems)
    for copy in copies:
        copy.start()
    wait_for(copies)


def own_window(own):
    return pl.pallas_call(
        own_kernel,
        out_shape=jax.ShapeDtypeStruct((BLOCK, own.shape[1] // 2 + 2 * PAD), own.dtype),
        in_specs=[ANY],
        out_specs=LOCAL,
        scratch_shapes=[pltpu.SemaphoreType.DMA((3,))],
        compiler_params=pltpu.CompilerParams(vmem_limit_bytes=SMALL),
        name="own_window",
    )(own)


def chip_kernel(piece, mate, out_ref, sems, piece_sem):
    row = pl.multiple_of((1 - core()) * BLOCK, BLOCK)
    copies = window_pieces(mate, out_ref, row, sems)
    own_row = pl.multiple_of(core() * BLOCK, BLOCK)
    copies.append(
        pltpu.make_async_copy(piece, out_ref.at[pl.ds(own_row, BLOCK), :], piece_sem)
    )
    for copy in copies:
        copy.start()
    wait_for(copies)


def chip_window(piece, mate):
    return pl.pallas_call(
        chip_kernel,
        out_shape=jax.ShapeDtypeStruct((2 * BLOCK, piece.shape[1]), piece.dtype),
        in_specs=[ANY, ANY],
        out_specs=LOCAL,
        scratch_shapes=[pltpu.SemaphoreType.DMA((3,)), pltpu.SemaphoreType.DMA],
        compiler_params=pltpu.CompilerParams(vmem_limit_bytes=SMALL),
        name="chip_window",
    )(piece, mate)


def join_kernel(got, whole, out, sem):
    half = whole.shape[1] // 2
    start = pl.multiple_of((1 - core()) * half, PAD)
    copy = pltpu.make_async_copy(got, out.at[:, pl.ds(start, half)], sem)
    copy.start()
    copy.wait()


def join(got, whole):
    return pl.pallas_call(
        join_kernel,
        out_shape=jax.ShapeDtypeStruct(whole.shape, whole.dtype),
        in_specs=[LOCAL, ANY],
        out_specs=ANY,
        scratch_shapes=[pltpu.SemaphoreType.DMA],
        input_output_aliases={1: 0},
        compiler_params=pltpu.CompilerParams(vmem_limit_bytes=VMEM),
        name="join",
    )(got, whole)


def in_parts(width):
    cut = width // 2 + PAD
    return ((0, cut), (cut, width - cut))


def chip_copies(blocks, width, x_ref, sems, start):
    cut = width // 2 + PAD
    return [
        [
            pltpu.make_async_copy(
                block.at[:, first : first + size],
                x_ref.at[
                    chip * 2 * BLOCK : (chip + 1) * 2 * BLOCK,
                    start + first : start + first + size,
                ],
                sems.at[at, chip],
            )
            for chip, block in enumerate(blocks)
        ]
        for at, (first, size) in enumerate(((0, cut), (cut, width - cut)))
    ]


def pre_shift(x_ref, x3_ref, first, size):
    for s in range(REACH):
        wide = x_ref[s * C : (s + 1) * C, first : first + size + 2 * PAD]
        for e in range(3):
            start = PAD + e - 1
            row = (3 * s + e) * C
            x3_ref[row : row + C, :] = wide[:, start : start + size]


def convolve(matrix_ref, x_ref, x3_ref, p3_ref, width, ready, finish):
    size = width // 2
    for tile in range(2):
        first = tile * size
        wait_for(ready[tile])
        pre_shift(x_ref, x3_ref.at[tile], first, size)
        for b in range(2):
            p3_ref[b * OUT : (b + 1) * OUT, first + PAD : first + PAD + size] = jnp.dot(
                matrix_ref[b * OUT : (b + 1) * OUT, :],
                x3_ref[tile, b * STEP : b * STEP + DEEP, :],
                preferred_element_type=jnp.float32,
            )
        finish(0 if tile == 0 else size - PAD, width if tile == 1 else size - PAD)


def post_shift(p3_ref, b, first, last):
    base = b * OUT
    total = p3_ref[base + BLOCK : base + 2 * BLOCK, first + PAD : last + PAD]
    for f in (0, 2):
        wide = p3_ref[base + f * BLOCK : base + (f + 1) * BLOCK, first : last + 2 * PAD]
        start = PAD + 3 * (f - 1)
        total = total + wide[:, start : start + last - first]
    return total


def forward_kernel(
    matrix_ref, table_ref, low, own, high, cot_own, cot_mate, out_ref, x_ref,
    x3_ref, p3_ref, cot_ref, sems, cot_sems,
):
    width = own.shape[1]
    copies = chip_copies((low, own, high), width, x_ref, sems, PAD)
    cot_copies = window_copies(cot_own, cot_mate, cot_ref, cot_sems)
    for copy in copies[0] + cot_copies + copies[1]:
        copy.start()

    def finish(first, last):
        if first == 0:
            wait_for(cot_copies)
        for b in range(2):
            rows = slice(b * BLOCK, (b + 1) * BLOCK)
            total = post_shift(p3_ref, b, first, last)
            cot = cot_ref[rows, first:last].astype(jnp.float32)
            sg = jax.nn.sigmoid(total)
            total = cot * sg * (1.0 + total * (1.0 - sg))
            out_ref[rows, first:last] = total.astype(out_ref.dtype)

    convolve(matrix_ref, x_ref, x3_ref, p3_ref, width, copies, finish)
    lane = lax.broadcasted_iota(jnp.int32, (C, LANES), 1)
    edge = out_ref[:C, :LANES].astype(jnp.float32)
    table = table_ref[...].astype(jnp.float32)
    table = jnp.where(lane < 3 * CHIP * TAPS, table, jnp.where(lane < PAD - RAD, 0.0, edge))
    out_ref[:C, :LANES] = table.astype(out_ref.dtype)


def conv_scratch(width):
    return [
        pltpu.VMEM((REACH * C, width + 2 * PAD), jnp.bfloat16),
        pltpu.VMEM((2, 3 * REACH * C, width // 2), jnp.bfloat16),
        pltpu.VMEM((2 * OUT, width + 2 * PAD), jnp.float32),
    ]


def work(width, arrays):
    return pl.CostEstimate(
        flops=4 * OUT * DEEP * width,
        bytes_accessed=arrays * 2 * BLOCK * width * 2,
        transcendentals=0,
    )


def forward(matrix, chip_table, blocks, cots):
    width = blocks[0].shape[1]
    return pl.pallas_call(
        forward_kernel,
        out_shape=(
            jax.ShapeDtypeStruct((2 * BLOCK, width), jnp.bfloat16),
            jax.ShapeDtypeStruct((REACH * C, width + 2 * PAD), jnp.bfloat16),
        ),
        in_specs=[LOCAL] * 2 + [ANY] * 5,
        out_specs=(LOCAL, LOCAL),
        scratch_shapes=conv_scratch(width)[1:]
        + [
            pltpu.VMEM((2 * BLOCK, width), jnp.bfloat16),
            pltpu.SemaphoreType.DMA((2, 3)),
            pltpu.SemaphoreType.DMA((2, 3)),
        ],
        compiler_params=pltpu.CompilerParams(vmem_limit_bytes=VMEM),
        cost_estimate=work(width, 5),
        name="forward_conv",
    )(matrix, chip_table, *blocks, *cots)


def input_filter(tables, weight_ref, matrix_ref, weight_wide, table_wide):
    weight_wide[...] = jnp.dot(
        weight_ref[...], spread_matrix("weight", (C, DEEP)), preferred_element_type=jnp.float32
    )
    row = lax.broadcasted_iota(jnp.int32, (3 * LANES, DEEP), 0)
    group = lax.broadcasted_iota(jnp.int32, (1, DEEP), 1) // C
    source = (group * 171) >> 9
    e = group - 3 * source
    for b in range(2):
        for q in range(OWN):
            whole = source + OWN * b
            tap = TAPS - 1 - source + q
            inside = jnp.logical_and(tap >= 0, tap < TAPS)
            wanted = (whole >> 2) * LANES + (whole & 3) * 3 * TAPS + 3 * tap + e
            wanted = jnp.where(inside, wanted, -1)
            picks = jnp.where(row == wanted, 1.0, 0.0).astype(jnp.bfloat16)
            table_wide[...] = jnp.dot(tables, picks, preferred_element_type=jnp.float32)
            for f in range(3):
                total = jnp.zeros((C, DEEP), jnp.float32)
                for k in range(K):
                    at = f * K + k
                    total = (
                        total
                        + table_wide[at : at + 1, :] * weight_wide[k * C : (k + 1) * C, :]
                    )
                first = b * OUT + f * BLOCK + q * C
                matrix_ref[first : first + C, :] = total.astype(jnp.bfloat16)


def backward_kernel(
    weight_ref, low, own, high, whole, give,
    x_ref, x3_ref, p3_ref, o_ref, t_ref, matrix_ref, weight_wide, table_wide,
    sems, table_sems, out_sems,
):
    width = own.shape[1]
    half = width - 2 * PAD
    table_copies = [
        pltpu.make_async_copy(
            block.at[0:C, 0:LANES],
            t_ref.at[:, chip * LANES : (chip + 1) * LANES],
            table_sems.at[chip],
        )
        for chip, block in enumerate((low, own, high))
    ]
    copies = chip_copies((low, own, high), width, x_ref, sems, PAD)
    for copy in table_copies + copies[0] + copies[1]:
        copy.start()
    wait_for(table_copies)
    input_filter(t_ref[...], weight_ref, matrix_ref, weight_wide, table_wide)

    def finish(first, last):
        first, last = max(first, PAD), min(last, width - PAD)
        for b in range(2):
            total = post_shift(p3_ref, b, first, last)
            o_ref[b * BLOCK : (b + 1) * BLOCK, first - PAD : last - PAD] = total.astype(
                o_ref.dtype
            )

    convolve(matrix_ref, x_ref, x3_ref, p3_ref, width, copies, finish)
    mine = pl.multiple_of(core() * BLOCK, BLOCK)
    other = pl.multiple_of((1 - core()) * BLOCK, BLOCK)
    column = pl.multiple_of(core() * half, PAD)
    sends = [
        pltpu.make_async_copy(o_ref.at[pl.ds(other, BLOCK), :], give, out_sems.at[0]),
        pltpu.make_async_copy(
            o_ref.at[pl.ds(mine, BLOCK), :], whole.at[:, pl.ds(column, half)], out_sems.at[1]
        ),
    ]
    for copy in sends:
        copy.start()
    wait_for(sends)


def backward(weights, low, own, high):
    width = own.shape[1]
    half = width - 2 * PAD
    return pl.pallas_call(
        backward_kernel,
        out_shape=(
            jax.ShapeDtypeStruct((BLOCK, 2 * half), jnp.bfloat16),
            jax.ShapeDtypeStruct((BLOCK, half), jnp.bfloat16),
        ),
        in_specs=[LOCAL] + [ANY] * 3,
        out_specs=(ANY, ANY),
        scratch_shapes=conv_scratch(width)
        + [
            pltpu.VMEM((2 * BLOCK, half), jnp.bfloat16),
            pltpu.VMEM((C, 3 * LANES), jnp.bfloat16),
            pltpu.VMEM((2 * OUT, DEEP), jnp.bfloat16),
            pltpu.VMEM((K * C, DEEP), jnp.float32),
            pltpu.VMEM((C, DEEP), jnp.float32),
            pltpu.SemaphoreType.DMA((2, 3)),
            pltpu.SemaphoreType.DMA((3,)),
            pltpu.SemaphoreType.DMA((2,)),
        ],
        compiler_params=pltpu.CompilerParams(vmem_limit_bytes=VMEM),
        cost_estimate=work(width, 4),
        name="input_conv",
    )(weights, low, own, high)


def weight_kernel(
    scale, x_ref, d_ref, table_ref, out_ref, x3_ref, d3_ref, g_ref, w_ref, table_wide
):
    width = d_ref.shape[1]
    size = width // 2 - PAD
    table_wide[...] = jnp.dot(
        table_ref[...],
        spread_matrix("table", (3 * SPAN, DEEP)),
        preferred_element_type=jnp.float32,
    )
    for tile in range(2):
        first = tile * size
        pre_shift(x_ref, x3_ref.at[tile], first + PAD, size)
        wide = d_ref[:, first : first + size + 2 * PAD]
        for f in range(3):
            start = PAD - 3 * (f - 1)
            for b in range(2):
                row = b * OUT + f * BLOCK
                d3_ref[tile, row : row + BLOCK, :] = wide[
                    b * BLOCK : (b + 1) * BLOCK, start : start + size
                ]
        for b in range(2):
            rows = slice(b * OUT, (b + 1) * OUT)
            product = lax.dot_general(
                d3_ref[tile, rows, :],
                x3_ref[tile, b * STEP : b * STEP + DEEP, :],
                (((1,), (1,)), ((), ())),
                preferred_element_type=jnp.float32,
            )
            if tile == 0:
                g_ref[rows, :] = product
            else:
                g_ref[rows, :] += product

    whole = DEEP // LANES
    for k in range(K):
        total = jnp.zeros((C, DEEP), jnp.float32)
        for group in range(3 * CHIP):
            at = group * K + k
            total = total + table_wide[at : at + 1, :] * g_ref[group * C : (group + 1) * C, :]
        narrow = jnp.concatenate(
            [total[:, whole * LANES :], jnp.zeros((C, (whole + 1) * LANES - DEEP), jnp.float32)],
            axis=1,
        )
        for part in range(whole):
            narrow = narrow + total[:, part * LANES : (part + 1) * LANES]
        w_ref[k * C : (k + 1) * C, :] = narrow
    row = lax.broadcasted_iota(jnp.int32, (LANES, LANES), 0)
    lane = lax.broadcasted_iota(jnp.int32, (LANES, LANES), 1)
    result = jnp.zeros((K * C // 4, LANES), jnp.float32)
    for c in range(4):
        fold = jnp.where(lane == c * C + row % C, 1.0, 0.0)
        result = result + jnp.dot(
            w_ref[pl.ds(c, K * C // 4, stride=4), :],
            fold,
            preferred_element_type=jnp.float32,
            precision=lax.Precision.HIGHEST,
        )
    out_ref[...] = result * scale


def weight_part(joined, delta, table, scale):
    width = delta.shape[1]
    return pl.pallas_call(
        functools.partial(weight_kernel, scale),
        out_shape=jax.ShapeDtypeStruct((K * C // 4, LANES), jnp.float32),
        in_specs=[LOCAL] * 3,
        out_specs=LOCAL,
        scratch_shapes=[
            pltpu.VMEM((2, 3 * REACH * C, width // 2 - PAD), jnp.bfloat16),
            pltpu.VMEM((2, 2 * OUT, width // 2 - PAD), jnp.bfloat16),
            pltpu.VMEM((2 * OUT, DEEP), jnp.float32),
            pltpu.VMEM((K * C, LANES), jnp.float32),
            pltpu.VMEM((3 * CHIP * K, DEEP), jnp.float32),
        ],
        compiler_params=pltpu.CompilerParams(vmem_limit_bytes=VMEM),
        cost_estimate=work(width, 4),
        name="weight_part",
    )(joined, delta, table)


def moved(array, by):
    peers = lax.axis_size("lat")
    return lax.ppermute(
        array, "lat", [(i, i + by) for i in range(peers) if 0 <= i + by < peers]
    )


def swapped(array, bit=1):
    return lax.ppermute(array, "lat", [(i, i ^ bit) for i in range(lax.axis_size("lat"))])


def summed(part, bits):
    if len(bits) == 1:
        return part + swapped(part, bits[0])
    one, two = bits
    others = [swapped(part, bit) for bit in (one, two, one + two)]
    return (part + others[0]) + (others[1] + others[2])


def as_table(padded):
    parts = padded.reshape(2, OWN, SPAN, 3, 3, K)
    return jnp.transpose(parts, (0, 3, 1, 5, 2, 4)).reshape(3 * CHIP * K, 3 * SPAN)


def forward_table(pair):
    rows = pair.reshape(2, OWN, TAPS, TAPS, K)
    return as_table(
        jnp.stack(
            [
                jnp.pad(rows[:, r], ((0, 0), (r, SPAN - TAPS - r), (0, 0), (0, 0)))
                for r in range(OWN)
            ],
            axis=1,
        )
    )


def sent_table(pair):
    parts = pair[:, :, ::-1].reshape(CHIP, TAPS, 3, 3, K)
    flat = jnp.transpose(parts, (2, 4, 0, 1, 3)).reshape(3 * K, 3 * CHIP * TAPS)
    return jnp.pad(flat, ((0, C - 3 * K), (0, LANES - 3 * CHIP * TAPS)))


def body(features, cotangent, basis_table, lon_reach, weights):
    longitude = features.shape[2]
    peers = lax.axis_size("lat")

    own = features.reshape(BLOCK, longitude)
    cot_own = cotangent.reshape(BLOCK, longitude)
    own_mate = swapped(own)

    offsets = jnp.arange(TAPS, dtype=jnp.int32) - RAD
    inside = jnp.abs(offsets)[None, None, :] <= lon_reach[:, :, None]
    masked = jnp.where(inside[..., None], basis_table, jnp.zeros_like(basis_table))
    mate = swapped(masked)
    pair = jnp.where(
        core() == 0, jnp.concatenate([masked, mate]), jnp.concatenate([mate, masked])
    )
    window = chip_window(own_window(own), own_mate)
    low, high = moved(window, 2), moved(window, -2)
    cot_mate = swapped(cot_own)

    table = forward_table(pair)
    matrix = make_filter(table, weights.reshape(K * C, C))
    delta, joined = forward(
        matrix, sent_table(pair), (low, window, high), (cot_own, cot_mate)
    )

    low, high = moved(delta, 2), moved(delta, -2)
    scale = 1.0 / math.sqrt(peers * OWN * longitude)
    total = weight_part(joined, delta, table, scale)
    for bits in ((1,), (32, 64)):
        total = summed(total, bits)
    low, high, total = lax.optimization_barrier((low, high, total))
    turned = jnp.transpose(weights, (0, 2, 1)).reshape(K * C, C)
    whole, give = backward(turned, low, delta, high)
    got = swapped(give)
    for bits in ((8, 16), (2, 4)):
        total = summed(total, bits)
    grad_input = join(got, whole)
    return grad_input.reshape(OWN, C, longitude), total.reshape(K, C, C)


def solution(mesh):
    in_specs = (
        P("lat", None, None),
        P("lat", None, None),
        P("lat", None, None, None),
        P("lat", None),
        P(),
    )
    out_specs = (P("lat", None, None), P())
    return jax.shard_map(body, mesh=mesh, in_specs=in_specs, out_specs=out_specs, check_vma=False)
```

```python
import functools
import math

import jax
import jax.numpy as jnp
from jax import lax
from jax.experimental import pallas as pl
from jax.experimental.pallas import tpu as pltpu
from jax.sharding import PartitionSpec as P

C = 32
K = 9
RAD = 4
TAPS = 9
OWN = 2
SPAN = OWN + 2 * RAD
CHIP = 2 * OWN
REACH = 3 * CHIP
BLOCK = OWN * C
STEP = 3 * BLOCK
DEEP = 3 * SPAN * C
OUT = 3 * BLOCK
PAD = 128
LANES = 128
VMEM = 26 * 1024 * 1024
SMALL = VMEM
LARGE = 58 * 1024 * 1024
ANY = pl.BlockSpec(memory_space=pl.ANY)
LOCAL = pl.BlockSpec(memory_space=pltpu.VMEM)


def core():
    return lax.rem(lax.axis_index("lat"), 2)


def spread_matrix(kind, shape):
    row = lax.broadcasted_iota(jnp.int32, shape, 0)
    lane = lax.broadcasted_iota(jnp.int32, shape, 1)
    hit = (lane // C == row) if kind == "table" else (lane % C == row)
    return jnp.where(hit, 1.0, 0.0).astype(jnp.bfloat16)


def filter_kernel(table_ref, weight_ref, out_ref, table_wide, weight_wide):
    table_wide[...] = jnp.dot(
        table_ref[...],
        spread_matrix("table", (3 * SPAN, DEEP)),
        preferred_element_type=jnp.float32,
    )
    weight_wide[...] = jnp.dot(
        weight_ref[...], spread_matrix("weight", (C, DEEP)), preferred_element_type=jnp.float32
    )
    for group in range(3 * CHIP):
        total = jnp.zeros((C, DEEP), jnp.float32)
        for k in range(K):
            at = group * K + k
            total = total + table_wide[at : at + 1, :] * weight_wide[k * C : (k + 1) * C, :]
        out_ref[group * C : (group + 1) * C, :] = total.astype(jnp.bfloat16)


def make_filter(table, weights):
    return pl.pallas_call(
        filter_kernel,
        out_shape=jax.ShapeDtypeStruct((2 * OUT, DEEP), jnp.bfloat16),
        in_specs=[LOCAL] * 2,
        out_specs=LOCAL,
        scratch_shapes=[
            pltpu.VMEM((3 * CHIP * K, DEEP), jnp.float32),
            pltpu.VMEM((K * C, DEEP), jnp.float32),
        ],
        compiler_params=pltpu.CompilerParams(vmem_limit_bytes=SMALL),
        name="make_filter",
    )(table, weights)


def wait_for(copies):
    for copy in copies:
        copy.wait()


def window_copies(own, mate, target, sems):
    longitude = own.shape[1]
    half = longitude // 2
    copies = []
    for side, (whole, place) in enumerate(((own, core()), (mate, 1 - core()))):
        row = pl.multiple_of(place * BLOCK, BLOCK)
        for at, (source, start, size) in enumerate(
            (
                (core() * half, PAD, half),
                (longitude - PAD - core() * half, 0, PAD),
                (half - core() * half, PAD + half, PAD),
            )
        ):
            copies.append(
                pltpu.make_async_copy(
                    whole.at[:, pl.ds(pl.multiple_of(source, PAD), size)],
                    target.at[pl.ds(row, BLOCK), pl.ds(start, size)],
                    sems.at[side, at],
                )
            )
    return copies


def window_pieces(whole, target, row, sems):
    longitude = whole.shape[1]
    half = longitude // 2
    return [
        pltpu.make_async_copy(
            whole.at[:, pl.ds(pl.multiple_of(source, PAD), size)],
            target.at[pl.ds(row, BLOCK), pl.ds(start, size)],
            sems.at[at],
        )
        for at, (source, start, size) in enumerate(
            (
                (core() * half, PAD, half),
                (longitude - PAD - core() * half, 0, PAD),
                (half - core() * half, PAD + half, PAD),
            )
        )
    ]


def own_kernel(own, out_ref, sems):
    copies = window_pieces(own, out_ref, 0, sems)
    for copy in copies:
        copy.start()
    wait_for(copies)


def own_window(own):
    return pl.pallas_call(
        own_kernel,
        out_shape=jax.ShapeDtypeStruct((BLOCK, own.shape[1] // 2 + 2 * PAD), own.dtype),
        in_specs=[ANY],
        out_specs=LOCAL,
        scratch_shapes=[pltpu.SemaphoreType.DMA((3,))],
        compiler_params=pltpu.CompilerParams(vmem_limit_bytes=SMALL),
        name="own_window",
    )(own)


def chip_kernel(piece, mate, out_ref, sems, piece_sem):
    row = pl.multiple_of((1 - core()) * BLOCK, BLOCK)
    copies = window_pieces(mate, out_ref, row, sems)
    own_row = pl.multiple_of(core() * BLOCK, BLOCK)
    copies.append(
        pltpu.make_async_copy(piece, out_ref.at[pl.ds(own_row, BLOCK), :], piece_sem)
    )
    for copy in copies:
        copy.start()
    wait_for(copies)


def chip_window(piece, mate):
    return pl.pallas_call(
        chip_kernel,
        out_shape=jax.ShapeDtypeStruct((2 * BLOCK, piece.shape[1]), piece.dtype),
        in_specs=[ANY, ANY],
        out_specs=LOCAL,
        scratch_shapes=[pltpu.SemaphoreType.DMA((3,)), pltpu.SemaphoreType.DMA],
        compiler_params=pltpu.CompilerParams(vmem_limit_bytes=SMALL),
        name="chip_window",
    )(piece, mate)


def join_kernel(got, whole, out, sem):
    half = whole.shape[1] // 2
    start = pl.multiple_of((1 - core()) * half, PAD)
    copy = pltpu.make_async_copy(got, out.at[:, pl.ds(start, half)], sem)
    copy.start()
    copy.wait()


def join(got, whole):
    return pl.pallas_call(
        join_kernel,
        out_shape=jax.ShapeDtypeStruct(whole.shape, whole.dtype),
        in_specs=[LOCAL, ANY],
        out_specs=ANY,
        scratch_shapes=[pltpu.SemaphoreType.DMA],
        input_output_aliases={1: 0},
        compiler_params=pltpu.CompilerParams(vmem_limit_bytes=VMEM),
        name="join",
    )(got, whole)


def in_parts(width):
    cut = width // 2 + PAD
    return ((0, cut), (cut, width - cut))


def chip_copies(blocks, width, x_ref, sems, start):
    cut = width // 2 + PAD
    return [
        [
            pltpu.make_async_copy(
                block.at[:, first : first + size],
                x_ref.at[
                    chip * 2 * BLOCK : (chip + 1) * 2 * BLOCK,
                    start + first : start + first + size,
                ],
                sems.at[at, chip],
            )
            for chip, block in enumerate(blocks)
        ]
        for at, (first, size) in enumerate(((0, cut), (cut, width - cut)))
    ]


def pre_shift(x_ref, x3_ref, first, size):
    for s in range(REACH):
        wide = x_ref[s * C : (s + 1) * C, first : first + size + 2 * PAD]
        for e in range(3):
            start = PAD + e - 1
            row = (3 * s + e) * C
            x3_ref[row : row + C, :] = wide[:, start : start + size]


def convolve(matrix_ref, x_ref, x3_ref, p3_ref, width, ready, finish):
    size = width // 2
    for tile in range(2):
        first = tile * size
        wait_for(ready[tile])
        pre_shift(x_ref, x3_ref.at[tile], first, size)
        for b in range(2):
            p3_ref[b * OUT : (b + 1) * OUT, first + PAD : first + PAD + size] = jnp.dot(
                matrix_ref[b * OUT : (b + 1) * OUT, :],
                x3_ref[tile, b * STEP : b * STEP + DEEP, :],
                preferred_element_type=jnp.float32,
            )
            finish(b, 0 if tile == 0 else size - PAD, width if tile == 1 else size - PAD)


def post_shift(p3_ref, b, first, last):
    base = b * OUT
    total = p3_ref[base + BLOCK : base + 2 * BLOCK, first + PAD : last + PAD]
    for f in (0, 2):
        wide = p3_ref[base + f * BLOCK : base + (f + 1) * BLOCK, first : last + 2 * PAD]
        start = PAD + 3 * (f - 1)
        total = total + wide[:, start : start + last - first]
    return total


def forward_kernel(
    matrix_ref, table_ref, low, own, high, cot_own, cot_mate, out_ref, x_ref,
    x3_ref, p3_ref, cot_ref, sems, cot_sems,
):
    width = own.shape[1]
    copies = chip_copies((low, own, high), width, x_ref, sems, PAD)
    cot_copies = window_copies(cot_own, cot_mate, cot_ref, cot_sems)
    for copy in copies[0] + cot_copies + copies[1]:
        copy.start()

    def finish(b, first, last):
        if first == 0 and b == 0:
            wait_for(cot_copies)
        rows = slice(b * BLOCK, (b + 1) * BLOCK)
        total = post_shift(p3_ref, b, first, last)
        cot = cot_ref[rows, first:last].astype(jnp.float32)
        sg = jax.nn.sigmoid(total)
        total = cot * sg * (1.0 + total * (1.0 - sg))
        out_ref[rows, first:last] = total.astype(out_ref.dtype)

    convolve(matrix_ref, x_ref, x3_ref, p3_ref, width, copies, finish)
    lane = lax.broadcasted_iota(jnp.int32, (C, LANES), 1)
    edge = out_ref[:C, :LANES].astype(jnp.float32)
    table = table_ref[...].astype(jnp.float32)
    table = jnp.where(lane < 3 * CHIP * TAPS, table, jnp.where(lane < PAD - RAD, 0.0, edge))
    out_ref[:C, :LANES] = table.astype(out_ref.dtype)


def conv_scratch(width):
    return [
        pltpu.VMEM((REACH * C, width + 2 * PAD), jnp.bfloat16),
        pltpu.VMEM((2, 3 * REACH * C, width // 2), jnp.bfloat16),
        pltpu.VMEM((2 * OUT, width + 2 * PAD), jnp.float32),
    ]


def work(width, arrays):
    return pl.CostEstimate(
        flops=4 * OUT * DEEP * width,
        bytes_accessed=arrays * 2 * BLOCK * width * 2,
        transcendentals=0,
    )


def forward(matrix, chip_table, blocks, cots):
    width = blocks[0].shape[1]
    return pl.pallas_call(
        forward_kernel,
        out_shape=(
            jax.ShapeDtypeStruct((2 * BLOCK, width), jnp.bfloat16),
            jax.ShapeDtypeStruct((REACH * C, width + 2 * PAD), jnp.bfloat16),
        ),
        in_specs=[LOCAL] * 2 + [ANY] * 5,
        out_specs=(LOCAL, LOCAL),
        scratch_shapes=conv_scratch(width)[1:]
        + [
            pltpu.VMEM((2 * BLOCK, width), jnp.bfloat16),
            pltpu.SemaphoreType.DMA((2, 3)),
            pltpu.SemaphoreType.DMA((2, 3)),
        ],
        compiler_params=pltpu.CompilerParams(vmem_limit_bytes=VMEM),
        cost_estimate=work(width, 5),
        name="forward_conv",
    )(matrix, chip_table, *blocks, *cots)


def input_filter(tables, weight_ref, matrix_ref, weight_wide, table_wide):
    weight_wide[...] = jnp.dot(
        weight_ref[...], spread_matrix("weight", (C, DEEP)), preferred_element_type=jnp.float32
    )
    row = lax.broadcasted_iota(jnp.int32, (3 * LANES, DEEP), 0)
    group = lax.broadcasted_iota(jnp.int32, (1, DEEP), 1) // C
    source = (group * 171) >> 9
    e = group - 3 * source
    for b in range(2):
        for q in range(OWN):
            whole = source + OWN * b
            tap = TAPS - 1 - source + q
            inside = jnp.logical_and(tap >= 0, tap < TAPS)
            wanted = (whole >> 2) * LANES + (whole & 3) * 3 * TAPS + 3 * tap + e
            wanted = jnp.where(inside, wanted, -1)
            picks = jnp.where(row == wanted, 1.0, 0.0).astype(jnp.bfloat16)
            table_wide[...] = jnp.dot(tables, picks, preferred_element_type=jnp.float32)
            for f in range(3):
                total = jnp.zeros((C, DEEP), jnp.float32)
                for k in range(K):
                    at = f * K + k
                    total = (
                        total
                        + table_wide[at : at + 1, :] * weight_wide[k * C : (k + 1) * C, :]
                    )
                first = b * OUT + f * BLOCK + q * C
                matrix_ref[first : first + C, :] = total.astype(jnp.bfloat16)


def backward_kernel(
    weight_ref, low, own, high, whole, give,
    x_ref, x3_ref, p3_ref, o_ref, t_ref, matrix_ref, weight_wide, table_wide,
    sems, table_sems, out_sems,
):
    width = own.shape[1]
    half = width - 2 * PAD
    table_copies = [
        pltpu.make_async_copy(
            block.at[0:C, 0:LANES],
            t_ref.at[:, chip * LANES : (chip + 1) * LANES],
            table_sems.at[chip],
        )
        for chip, block in enumerate((low, own, high))
    ]
    copies = chip_copies((low, own, high), width, x_ref, sems, PAD)
    for copy in table_copies + copies[0] + copies[1]:
        copy.start()
    wait_for(table_copies)
    input_filter(t_ref[...], weight_ref, matrix_ref, weight_wide, table_wide)

    def finish(b, first, last):
        first, last = max(first, PAD), min(last, width - PAD)
        total = post_shift(p3_ref, b, first, last)
        o_ref[b * BLOCK : (b + 1) * BLOCK, first - PAD : last - PAD] = total.astype(o_ref.dtype)

    convolve(matrix_ref, x_ref, x3_ref, p3_ref, width, copies, finish)
    mine = pl.multiple_of(core() * BLOCK, BLOCK)
    other = pl.multiple_of((1 - core()) * BLOCK, BLOCK)
    column = pl.multiple_of(core() * half, PAD)
    sends = [
        pltpu.make_async_copy(o_ref.at[pl.ds(other, BLOCK), :], give, out_sems.at[0]),
        pltpu.make_async_copy(
            o_ref.at[pl.ds(mine, BLOCK), :], whole.at[:, pl.ds(column, half)], out_sems.at[1]
        ),
    ]
    for copy in sends:
        copy.start()
    wait_for(sends)


def backward(weights, low, own, high):
    width = own.shape[1]
    half = width - 2 * PAD
    return pl.pallas_call(
        backward_kernel,
        out_shape=(
            jax.ShapeDtypeStruct((BLOCK, 2 * half), jnp.bfloat16),
            jax.ShapeDtypeStruct((BLOCK, half), jnp.bfloat16),
        ),
        in_specs=[LOCAL] + [ANY] * 3,
        out_specs=(ANY, ANY),
        scratch_shapes=conv_scratch(width)
        + [
            pltpu.VMEM((2 * BLOCK, half), jnp.bfloat16),
            pltpu.VMEM((C, 3 * LANES), jnp.bfloat16),
            pltpu.VMEM((2 * OUT, DEEP), jnp.bfloat16),
            pltpu.VMEM((K * C, DEEP), jnp.float32),
            pltpu.VMEM((C, DEEP), jnp.float32),
            pltpu.SemaphoreType.DMA((2, 3)),
            pltpu.SemaphoreType.DMA((3,)),
            pltpu.SemaphoreType.DMA((2,)),
        ],
        compiler_params=pltpu.CompilerParams(vmem_limit_bytes=VMEM),
        cost_estimate=work(width, 4),
        name="input_conv",
    )(weights, low, own, high)


def weight_kernel(
    scale, x_ref, d_ref, table_ref, out_ref, x3_ref, d3_ref, g_ref, w_ref, table_wide
):
    width = d_ref.shape[1]
    size = width // 2 - PAD
    table_wide[...] = jnp.dot(
        table_ref[...],
        spread_matrix("table", (3 * SPAN, DEEP)),
        preferred_element_type=jnp.float32,
    )
    for tile in range(2):
        first = tile * size
        pre_shift(x_ref, x3_ref.at[tile], first + PAD, size)
        wide = d_ref[:, first : first + size + 2 * PAD]
        for f in range(3):
            start = PAD - 3 * (f - 1)
            for b in range(2):
                row = b * OUT + f * BLOCK
                d3_ref[tile, row : row + BLOCK, :] = wide[
                    b * BLOCK : (b + 1) * BLOCK, start : start + size
                ]
        for b in range(2):
            rows = slice(b * OUT, (b + 1) * OUT)
            product = lax.dot_general(
                d3_ref[tile, rows, :],
                x3_ref[tile, b * STEP : b * STEP + DEEP, :],
                (((1,), (1,)), ((), ())),
                preferred_element_type=jnp.float32,
            )
            if tile == 0:
                g_ref[rows, :] = product
            else:
                g_ref[rows, :] += product

    whole = DEEP // LANES
    for k in range(K):
        total = jnp.zeros((C, DEEP), jnp.float32)
        for group in range(3 * CHIP):
            at = group * K + k
            total = total + table_wide[at : at + 1, :] * g_ref[group * C : (group + 1) * C, :]
        narrow = jnp.concatenate(
            [total[:, whole * LANES :], jnp.zeros((C, (whole + 1) * LANES - DEEP), jnp.float32)],
            axis=1,
        )
        for part in range(whole):
            narrow = narrow + total[:, part * LANES : (part + 1) * LANES]
        w_ref[k * C : (k + 1) * C, :] = narrow
    row = lax.broadcasted_iota(jnp.int32, (LANES, LANES), 0)
    lane = lax.broadcasted_iota(jnp.int32, (LANES, LANES), 1)
    result = jnp.zeros((K * C // 4, LANES), jnp.float32)
    for c in range(4):
        fold = jnp.where(lane == c * C + row % C, 1.0, 0.0)
        result = result + jnp.dot(
            w_ref[pl.ds(c, K * C // 4, stride=4), :],
            fold,
            preferred_element_type=jnp.float32,
            precision=lax.Precision.HIGHEST,
        )
    out_ref[...] = result * scale


def weight_part(joined, delta, table, scale):
    width = delta.shape[1]
    return pl.pallas_call(
        functools.partial(weight_kernel, scale),
        out_shape=jax.ShapeDtypeStruct((K * C // 4, LANES), jnp.float32),
        in_specs=[LOCAL] * 3,
        out_specs=LOCAL,
        scratch_shapes=[
            pltpu.VMEM((2, 3 * REACH * C, width // 2 - PAD), jnp.bfloat16),
            pltpu.VMEM((2, 2 * OUT, width // 2 - PAD), jnp.bfloat16),
            pltpu.VMEM((2 * OUT, DEEP), jnp.float32),
            pltpu.VMEM((K * C, LANES), jnp.float32),
            pltpu.VMEM((3 * CHIP * K, DEEP), jnp.float32),
        ],
        compiler_params=pltpu.CompilerParams(vmem_limit_bytes=VMEM),
        cost_estimate=work(width, 4),
        name="weight_part",
    )(joined, delta, table)


def moved(array, by):
    peers = lax.axis_size("lat")
    return lax.ppermute(
        array, "lat", [(i, i + by) for i in range(peers) if 0 <= i + by < peers]
    )


def swapped(array, bit=1):
    return lax.ppermute(array, "lat", [(i, i ^ bit) for i in range(lax.axis_size("lat"))])


def summed(part, bits):
    if len(bits) == 1:
        return part + swapped(part, bits[0])
    one, two = bits
    others = [swapped(part, bit) for bit in (one, two, one + two)]
    return (part + others[0]) + (others[1] + others[2])


def as_table(padded):
    parts = padded.reshape(2, OWN, SPAN, 3, 3, K)
    return jnp.transpose(parts, (0, 3, 1, 5, 2, 4)).reshape(3 * CHIP * K, 3 * SPAN)


def forward_table(pair):
    rows = pair.reshape(2, OWN, TAPS, TAPS, K)
    return as_table(
        jnp.stack(
            [
                jnp.pad(rows[:, r], ((0, 0), (r, SPAN - TAPS - r), (0, 0), (0, 0)))
                for r in range(OWN)
            ],
            axis=1,
        )
    )


def sent_table(pair):
    parts = pair[:, :, ::-1].reshape(CHIP, TAPS, 3, 3, K)
    flat = jnp.transpose(parts, (2, 4, 0, 1, 3)).reshape(3 * K, 3 * CHIP * TAPS)
    return jnp.pad(flat, ((0, C - 3 * K), (0, LANES - 3 * CHIP * TAPS)))


def body(features, cotangent, basis_table, lon_reach, weights):
    longitude = features.shape[2]
    peers = lax.axis_size("lat")

    own = features.reshape(BLOCK, longitude)
    cot_own = cotangent.reshape(BLOCK, longitude)
    own_mate = swapped(own)

    offsets = jnp.arange(TAPS, dtype=jnp.int32) - RAD
    inside = jnp.abs(offsets)[None, None, :] <= lon_reach[:, :, None]
    masked = jnp.where(inside[..., None], basis_table, jnp.zeros_like(basis_table))
    mate = swapped(masked)
    pair = jnp.where(
        core() == 0, jnp.concatenate([masked, mate]), jnp.concatenate([mate, masked])
    )
    window = chip_window(own_window(own), own_mate)
    low, high = moved(window, 2), moved(window, -2)
    cot_mate = swapped(cot_own)

    table = forward_table(pair)
    matrix = make_filter(table, weights.reshape(K * C, C))
    delta, joined = forward(
        matrix, sent_table(pair), (low, window, high), (cot_own, cot_mate)
    )

    low, high = moved(delta, 2), moved(delta, -2)
    scale = 1.0 / math.sqrt(peers * OWN * longitude)
    total = weight_part(joined, delta, table, scale)
    for bits in ((1,), (32, 64)):
        total = summed(total, bits)
    low, high, total = lax.optimization_barrier((low, high, total))
    turned = jnp.transpose(weights, (0, 2, 1)).reshape(K * C, C)
    whole, give = backward(turned, low, delta, high)
    got = swapped(give)
    for bits in ((8, 16), (2, 4)):
        total = summed(total, bits)
    grad_input = join(got, whole)
    return grad_input.reshape(OWN, C, longitude), total.reshape(K, C, C)


def solution(mesh):
    in_specs = (
        P("lat", None, None),
        P("lat", None, None),
        P("lat", None, None, None),
        P("lat", None),
        P(),
    )
    out_specs = (P("lat", None, None), P())
    return jax.shard_map(body, mesh=mesh, in_specs=in_specs, out_specs=out_specs, check_vma=False)
```
